256 devices in a mesh: seq: 128 (over x_lo, z, y, core), head: 2 (over x_hi).
Axes of the slice: x: 4 (x_hi: 2, x_lo: 2; x = x_hi * 2 + x_lo), y: 4, z: 8, core: 2. Of those that a mesh axis runs over, the one named last changes fastest.
Arguments:
- tokens: bfloat16 [32768, 1536], P('seq', 'head'), may hold values from -8 to 8
- w_qkv: bfloat16 [1536, 3, 768], P(None, None, 'head'), may hold values from -0.15625 to 0.15625
- w_out: bfloat16 [768, 1536], P('head'), may hold values from -0.21875 to 0.21875
- grad_out: bfloat16 [32768, 1536], P('seq', 'head'), may hold values from -24 to 24
- offsets: int32 [4, 12], P(None, 'head'), may hold values from 0 to 255, as said below
Outputs:
- mixed: bfloat16 [32768, 1536], P('seq', 'head')
- grad_tokens: bfloat16 [32768, 1536], P('seq', 'head')
- grad_qkv: float32 [1536, 3, 768], P('seq', None, 'head')
- grad_w_out: float32 [768, 1536], P('head', 'seq')
The draws below stay inside these ranges and needn't reach their ends.
Inputs may be any that keep to these rules, and one draw needn't show every extreme that they name: offsets[l, h] is below the dilation r_l of level l (1, 4, 64, 256); at every level some head takes r_l - 1.
All inputs are finite; a program needn't handle non-finite values.
Results may differ from the reference program's by a relative error of at most 0.017.
Values may be sent and summed in bfloat16 or wider, within the bound.
A program may use at most 128 MiB of HBM per device.

```python
import jax
import jax.numpy as jnp
from jax import lax

D = 1536
HEADS = 12
HDIM = 64
LEVELS = 4
TOK_DEV = 256
TOKENS = 32768
N_SEQ = 128


def draw_offsets(key, part):
    key = jax.random.fold_in(key, 7)
    first, second = jax.random.split(key, 2)
    dilations = jnp.array([1, 4, N_SEQ // 2, 2 * N_SEQ], jnp.int32)
    raw = jax.random.randint(first, (LEVELS, HEADS), 0, 1 << 30, dtype=jnp.int32)
    base = raw % dilations[:, None]
    chosen = jax.random.randint(second, (LEVELS, 1), 0, HEADS, dtype=jnp.int32)
    marked = jnp.arange(HEADS, dtype=jnp.int32)[None, :] == chosen
    return jnp.where(marked, dilations[:, None] - 1, base).astype(jnp.int32)


def with_spikes(entries, key, source, target, shards_of, factor):
    def block_of(axis_at):
        return (jnp.arange(entries.shape[axis_at]) // (entries.shape[axis_at] // shards_of)).reshape((-1,) + (1,) * (entries.ndim - 1 - axis_at))

    near = jax.random.permutation(key, shards_of)[block_of(target)]
    other_side = (block_of(target) + shards_of // 2) % shards_of
    return jnp.where((block_of(source) == near) | (block_of(source) == other_side), factor * entries, entries)


def steps_of(own_key, extent, cuts, low, top_value):
    gain, own = 1.0, jax.random.fold_in(own_key, 6)
    for position, shards_of in cuts:
        steps = jnp.exp(jax.random.uniform(jax.random.fold_in(own, position), (shards_of,), jnp.float32, low / len(cuts), top_value / len(cuts)))
        gain = gain * jnp.repeat(steps, extent[position] // shards_of).reshape([-1 if axis == position else 1 for axis in range(len(extent))])
    return gain


def gaussian(rng, dims, scale, most, shards=(), kind=jnp.bfloat16):
    values = scale * jax.random.normal(rng, dims, jnp.float32)
    if shards:
        values = values * steps_of(rng, dims, shards, -0.22, 0.18)
    return jnp.clip(values, -most, most).astype(kind)


def heavy_noise(stream_key, dims, spread, limit, shards, heavy, kind=jnp.bfloat16):
    drawn = spread * jax.random.normal(stream_key, dims, jnp.float32)
    if shards:
        drawn = drawn * steps_of(stream_key, dims, shards, -0.22, 0.18)
    return jnp.clip(with_spikes(drawn, jax.random.fold_in(stream_key, 3), *heavy), -limit, limit).astype(kind)


def setup_inputs(seed: int = 0) -> dict:
    key_of = jax.random.split(jax.random.key(seed), 6)
    tokens = heavy_noise(key_of[0], (TOKENS, D), 0.7, 8.0, ((0, 128), (1, 2)), (0, 1, 128, 5.5))
    w_qkv = gaussian(key_of[1], (D, 3, HEADS * HDIM), D ** -0.5, 0.15625, ((2, 2),))
    w_out = gaussian(key_of[2], (HEADS * HDIM, D), (HEADS * HDIM) ** -0.5, 0.21875, ((0, 2),))
    grad_out = heavy_noise(key_of[3], (TOKENS, D), 1.0, 24.0, ((0, 128), (1, 2)), (0, 1, 128, 5.5))
    offsets = draw_offsets(jax.random.fold_in(key_of[5], 71), 0)
    return dict(tokens=tokens, w_qkv=w_qkv, w_out=w_out, grad_out=grad_out, offsets=offsets)


SCALE = 0.125


def level_table():
    return [(1, 1), (4, 4), (N_SEQ // 2, N_SEQ // 2), (N_SEQ, 2 * N_SEQ)]


def select_rows(values, dilation, shifts):
    length, heads, inner = values.shape
    blocks = values.reshape(length // dilation, dilation, heads, inner)
    index = jnp.broadcast_to(shifts.astype(jnp.int32)[None, None, :, None], (length // dilation, 1, heads, inner))
    return jnp.take_along_axis(blocks, index, axis=1)[:, 0]


def spread_rows(picked, dilation, shifts):
    count, heads, inner = picked.shape
    hit = jnp.arange(dilation, dtype=jnp.int32)[None, :, None, None] == shifts.astype(jnp.int32)[None, None, :, None]
    full = jnp.where(hit, picked[:, None], jnp.zeros((), picked.dtype))
    return full.reshape(count * dilation, heads, inner)


def rounded(values):
    return lax.optimization_barrier(values.astype(jnp.bfloat16)).astype(jnp.float32)


def attend_forward(queries, keys, values):
    scores = jnp.einsum('qhe,khe->hqk', queries.astype(jnp.float32), keys.astype(jnp.float32)) * SCALE
    weights = jnp.exp(scores)
    total = jnp.sum(weights, axis=2)
    numer = jnp.einsum('hqk,khe->qhe', rounded(weights), values.astype(jnp.float32))
    return numer, jnp.transpose(total)[:, :, None]


def attend_backward(queries, keys, values, grads, deltas, totals):
    scores = jnp.einsum('qhe,khe->hqk', queries.astype(jnp.float32), keys.astype(jnp.float32)) * SCALE
    probs = jnp.exp(scores) / jnp.transpose(totals, (1, 0, 2))
    grad_values = jnp.einsum('hqk,qhe->khe', rounded(probs), grads.astype(jnp.float32))
    grad_probs = jnp.einsum('qhe,khe->hqk', grads.astype(jnp.float32), values.astype(jnp.float32))
    grad_scores = rounded(probs * (grad_probs - jnp.transpose(deltas, (1, 0, 2))))
    grad_queries = jnp.einsum('hqk,khe->qhe', grad_scores, keys.astype(jnp.float32)) * SCALE
    grad_keys = jnp.einsum('hqk,qhe->khe', grad_scores, queries.astype(jnp.float32)) * SCALE
    return grad_queries, grad_keys, grad_values


def reference(tokens, w_qkv, w_out, grad_out, offsets):
    length = TOKENS
    width = HEADS * HDIM
    weight_flat = w_qkv.reshape(D, 3 * width)
    projected = jnp.dot(tokens, weight_flat, preferred_element_type=jnp.float32).astype(jnp.bfloat16)
    projected = projected.reshape(length, 3, HEADS, HDIM)
    queries, keys, values = projected[:, 0], projected[:, 1], projected[:, 2]
    numer = jnp.zeros((length, HEADS, HDIM), jnp.float32)
    denom = jnp.zeros((length, HEADS, 1), jnp.float32)
    for level, (group, dilation) in enumerate(level_table()):
        shifts = offsets[level]
        segments = N_SEQ // group
        seg_rows = group * TOK_DEV // dilation

        def cut(array):
            return select_rows(array, dilation, shifts).reshape(segments, seg_rows, HEADS, array.shape[-1])

        part_num, part_den = lax.map(lambda item: attend_forward(*item), (cut(queries), cut(keys), cut(values)))
        numer = numer + spread_rows(part_num.reshape(segments * seg_rows, HEADS, HDIM), dilation, shifts)
        denom = denom + spread_rows(part_den.reshape(segments * seg_rows, HEADS, 1), dilation, shifts)
    attended = (numer / denom).astype(jnp.bfloat16)
    flat = attended.reshape(length, width)
    mixed = jnp.dot(flat, w_out, preferred_element_type=jnp.float32).astype(jnp.bfloat16)
    grad_w_out = jnp.dot(flat.T, grad_out, preferred_element_type=jnp.float32)
    grad_att = jnp.dot(grad_out, w_out.T, preferred_element_type=jnp.float32).astype(jnp.bfloat16)
    grad_att = grad_att.reshape(length, HEADS, HDIM)
    deltas = jnp.sum(grad_att.astype(jnp.float32) * attended.astype(jnp.float32), axis=2, keepdims=True)
    grad_q = jnp.zeros((length, HEADS, HDIM), jnp.float32)
    grad_k = jnp.zeros((length, HEADS, HDIM), jnp.float32)
    grad_v = jnp.zeros((length, HEADS, HDIM), jnp.float32)
    for level, (group, dilation) in enumerate(level_table()):
        shifts = offsets[level]
        segments = N_SEQ // group
        seg_rows = group * TOK_DEV // dilation

        def cut(array):
            return select_rows(array, dilation, shifts).reshape(segments, seg_rows, HEADS, array.shape[-1])

        part_q, part_k, part_v = lax.map(lambda item: attend_backward(*item), (cut(queries), cut(keys), cut(values), cut(grad_att), cut(deltas), cut(denom)))
        grad_q = grad_q + spread_rows(part_q.reshape(segments * seg_rows, HEADS, HDIM), dilation, shifts)
        grad_k = grad_k + spread_rows(part_k.reshape(segments * seg_rows, HEADS, HDIM), dilation, shifts)
        grad_v = grad_v + spread_rows(part_v.reshape(segments * seg_rows, HEADS, HDIM), dilation, shifts)
    grads_qkv = jnp.stack([grad_q.astype(jnp.bfloat16), grad_k.astype(jnp.bfloat16), grad_v.astype(jnp.bfloat16)], axis=1)
    grads_qkv = grads_qkv.reshape(length, 3 * width)
    grad_tokens = jnp.dot(grads_qkv, weight_flat.T, preferred_element_type=jnp.float32).astype(jnp.bfloat16)
    grad_qkv = jnp.dot(tokens.T, grads_qkv, preferred_element_type=jnp.float32).reshape(D, 3, width)
    return mixed, grad_tokens, grad_qkv, grad_w_out
```

```python
import jax
import jax.numpy as jnp
import numpy as np
from jax import lax
from jax.experimental import pallas as pl
from jax.experimental.pallas import tpu as pltpu
from jax.sharding import PartitionSpec as P

MESH = pl.DeviceIdType.MESH
BF = jnp.bfloat16
F32 = jnp.float32
ROWS = 256
WIDTH = 384
HALF = 768
HEADS = 6
SCALE = 0.125

NN = (((1,), (0,)), ((), ()))
NT = (((1,), (1,)), ((), ()))
TN = (((0,), (0,)), ((), ()))


def mm(a, b, dims=NN):
    return lax.dot_general(a, b, dims, preferred_element_type=F32)


def iota(shape, dim):
    return lax.broadcasted_iota(jnp.int32, shape, dim)


def halves(x):
    high = x.astype(BF)
    return high, (x - high.astype(F32)).astype(BF)


def place(spread, x):
    high, low = halves(x)
    return mm(spread, high) + mm(spread, low)


def by_head(pieces):
    lanes = iota((1, pieces[0].shape[1]), 1)
    lanes = jnp.where(lanes >= WIDTH, lanes - WIDTH, lanes)
    out = pieces[0]
    for h in range(1, HEADS):
        out = jnp.where(lanes >= 64 * h, pieces[h], out)
    return out


def block_mask(rows_per_head):
    rows = HEADS * rows_per_head
    head = iota((rows, WIDTH), 0) // rows_per_head
    return head == iota((rows, WIDTH), 1) // 64


def level_forward(q_block, keys, values, own_lanes, mask):
    weights = jnp.exp(mm(q_block, keys, NT))
    if mask is not None:
        weights = jnp.where(mask, weights, 0.0)
    total = jnp.sum(weights, axis=1, keepdims=True)
    numer = mm(weights.astype(BF), values)
    both = jnp.concatenate(
        [jnp.where(own_lanes, numer, 0.0), jnp.where(own_lanes, total, 0.0)], 1
    )
    return weights, both


def level_backward(weights, q_block, grad_block, keys, values, inverse, delta, own_lanes):
    probs = weights * inverse
    grad_probs = mm(grad_block, values, NT)
    grad_scores = (probs * (grad_probs - delta)).astype(BF)
    grad_values = mm(probs.astype(BF), grad_block, TN)
    grad_keys = mm(grad_scores, q_block, TN)
    grad_q = jnp.where(own_lanes, mm(grad_scores, keys) * SCALE, 0.0)
    return grad_q, jnp.concatenate([grad_keys, grad_values], 1)


def kernel(
    tok_hbm, gout_hbm, wqkv_hbm, wout_hbm, perm_hbm, comp_hbm, off_ref,
    mixed_ref, gtok_ref, gqkv_ref, gwout_ref,
    tok, gout, wqkv, wout, perm, comp, sib_tok, sib_gout,
    acc, qkv, kv1, s1, kv23, w0, w1, w23, numer_ref, den_ref, gatt, att_buf, gq_acc, gkv_acc,
    tok_t, gout_t, gbuf, gsend1, grecv1, gsendz, grecvz, gsends, grecvs,
    mixed_out, mixed_in, gtok_out, gtok_in,
    ysend, yrecv, zsend, zrecv, xbuf, xrecv,
    local_sem, head_s, head_r, sib_s, sib_r, k1_s, k1_r, s1_s, s1_r, kz_s, kz_r,
    r1_s, r1_r, rz_s, rz_r, rs_s, rs_r, y_s, y_r, z_s, z_r, x_s, x_r,
):
    seq = lax.axis_index("seq")
    head = lax.axis_index("head")

    def bit(step):
        return lax.rem(lax.div(seq, step), 2)

    core = bit(1)
    y_at = lax.rem(lax.div(seq, 2), 4)
    z_at = lax.rem(lax.div(seq, 8), 8)
    x_at = lax.div(seq, 64)

    def flipped(d, steps):
        other = seq
        for b, step in enumerate(steps):
            if d >> b & 1:
                other = other + (1 - 2 * bit(step)) * step
        return other

    group_steps = (1, 2, 4, 64)
    z_steps = (8, 16, 32)
    group_peer = [flipped(d, group_steps) for d in range(16)]
    z_peer = [flipped(d, z_steps) for d in range(8)]
    y_peer = [flipped(d, (2, 4)) for d in range(4)]
    sibling = group_peer[1]
    other_head = 1 - head

    def push(src, dst, send, recv, to_seq, to_head=None):
        target = (to_seq, head if to_head is None else to_head)
        copy = pltpu.make_async_remote_copy(
            src_ref=src, dst_ref=dst, send_sem=send, recv_sem=recv,
            device_id=target, device_id_type=MESH,
        )
        copy.start()
        sent.append(copy)
        return copy

    sent = []

    loads = []
    for n, (src, dst) in enumerate([
        (tok_hbm, tok.at[head]), (wqkv_hbm, wqkv), (gout_hbm, gout.at[head]),
        (wout_hbm, wout), (comp_hbm, comp), (perm_hbm, perm),
    ]):
        copy = pltpu.make_async_copy(src, dst, local_sem.at[n])
        copy.start()
        loads.append(copy)

    barrier = pltpu.get_barrier_semaphore()
    peers = [(seq, other_head)]
    peers += [(group_peer[d], head) for d in range(1, 16)]
    peers += [(z_peer[d], head) for d in range(1, 8)]
    for peer in peers:
        pl.semaphore_signal(barrier, inc=1, device_id=peer, device_id_type=MESH)
    pl.semaphore_wait(barrier, len(peers))

    tok_copy = push(tok_hbm, tok.at[head], head_s.at[0], head_r.at[0], seq, other_head)
    gout_copy = push(gout_hbm, gout.at[head], head_s.at[1], head_r.at[1], seq, other_head)

    loads[0].wait()
    loads[1].wait()
    for j in range(3):
        cols = slice(WIDTH * j, WIDTH * (j + 1))
        acc[:, cols] = mm(tok[head], wqkv[j, pl.ds(pl.multiple_of(head * HALF, HALF), HALF), :])

    lane = iota((64, ROWS), 1)
    row = iota((64, ROWS), 0)
    pick1 = jnp.concatenate(
        [jnp.where(lane == 4 * row + off_ref[1, h], 1.0, 0.0) for h in range(HEADS)], 0
    ).astype(BF)
    lane8 = iota((8, ROWS), 1)
    row8 = iota((8, ROWS), 0)

    def spot(at, h):
        return jnp.where(
            at < 4, 64 * at + off_ref[2, h], jnp.where(at == 4, off_ref[3, h], -1)
        )

    pick23 = jnp.concatenate(
        [jnp.where(lane8 == spot(row8, h), 1.0, 0.0) for h in range(HEADS)], 0
    ).astype(BF)
    at1 = iota((1, WIDTH), 1)
    spot1 = 4 * at1 + off_ref[1, 0]
    for h in range(1, HEADS):
        spot1 = jnp.where(at1 >= 64 * h, 4 * (at1 - 64 * h) + off_ref[1, h], spot1)
    put1 = jnp.where(iota((ROWS, WIDTH), 0) == spot1, 1.0, 0.0).astype(BF)
    at23 = iota((1, 8 * HEADS), 1)
    spot23 = spot(at23, 0)
    for h in range(1, HEADS):
        spot23 = jnp.where(at23 >= 8 * h, spot(at23 - 8 * h, h), spot23)
    put23 = jnp.where(iota((ROWS, 8 * HEADS), 0) == spot23, 1.0, 0.0).astype(BF)
    own1 = block_mask(64)
    own23 = block_mask(8)

    tok_copy.wait_recv()
    for j in range(3):
        cols = slice(WIDTH * j, WIDTH * (j + 1))
        other_rows = pl.ds(pl.multiple_of(other_head * HALF, HALF), HALF)
        part = acc[:, cols] + mm(tok[other_head], wqkv[j, other_rows, :])
        if j == 0:
            part = part.astype(BF).astype(F32) * SCALE
        qkv[:, cols] = part.astype(BF)

    key_value = qkv[:, WIDTH:]
    picked23 = mm(pick23, key_value)
    small = by_head([picked23[8 * h : 8 * h + 8] for h in range(HEADS)])
    s1[0] = jnp.concatenate([small, jnp.zeros_like(small)], 0).astype(BF)
    s1_copies = [
        push(s1.at[0], s1.at[d], s1_s.at[d], s1_r.at[d], group_peer[d]) for d in range(1, 16)
    ]
    picked1 = mm(pick1, key_value)
    kv1[0] = by_head([picked1[64 * h : 64 * h + 64] for h in range(HEADS)]).astype(BF)
    k1_copies = [
        push(kv1.at[0], kv1.at[d], k1_s.at[d], k1_r.at[d], group_peer[d]) for d in range(1, 4)
    ]
    sib_tok_copy = push(tok.at[1 - core], sib_tok, sib_s.at[0], sib_r.at[0], sibling)

    q_block1 = jnp.where(own1, mm(pick1, qkv[:, :WIDTH]), 0.0).astype(BF)
    q_block23 = jnp.where(own23, mm(pick23, qkv[:, :WIDTH]), 0.0).astype(BF)

    low_lanes = iota((1, 128), 1) < 64
    side = [jnp.where(low_lanes, 1.0, 0.0).astype(BF), jnp.where(low_lanes, 0.0, 1.0).astype(BF)]

    def pair(start, p):
        return qkv[:, start + 128 * p : start + 128 * p + 128]

    def level0_forward(p):
        queries, keys, values = pair(0, p), pair(WIDTH, p), pair(2 * WIDTH, p)
        parts = []
        for e in range(2):
            weights = jnp.exp(mm(queries * side[e], keys, NT))
            w0[2 * p + e] = weights
            parts.append((mm(weights.astype(BF), values), jnp.sum(weights, axis=1, keepdims=True)))
        numer_ref[:, 128 * p : 128 * p + 128] = jnp.where(low_lanes, parts[0][0], parts[1][0])
        den_ref[:, 128 * p : 128 * p + 128] = jnp.where(low_lanes, parts[0][1], parts[1][1])

    level0_forward(0)

    loads[4].wait()
    for copy in s1_copies:
        copy.wait_recv()
    kv23[0] = mm(comp[...], s1[...].reshape(256, 2 * WIDTH)).astype(BF)
    kz_copies = [
        push(kv23.at[0], kv23.at[d], kz_s.at[d], kz_r.at[d], z_peer[d]) for d in range(1, 8)
    ]

    level0_forward(1)
    level0_forward(2)

    loads[2].wait()
    loads[3].wait()
    gout_copy.wait_recv()
    sib_gout_copy = push(gout.at[1 - core], sib_gout, sib_s.at[1], sib_r.at[1], sibling)
    grad_att = (mm(gout[0], wout[:, :HALF], NT) + mm(gout[1], wout[:, HALF:], NT)).astype(BF)
    gatt[...] = grad_att
    g_block1 = jnp.where(own1, mm(pick1, grad_att), 0.0).astype(BF)
    g_block23 = jnp.where(own23, mm(pick23, grad_att), 0.0).astype(BF)

    for copy in k1_copies:
        copy.wait_recv()
    keys1, values1 = kv1[:, :, :WIDTH].reshape(256, WIDTH), kv1[:, :, WIDTH:].reshape(256, WIDTH)
    weights, both = level_forward(q_block1, keys1, values1, own1, None)
    w1[...] = weights
    placed = place(put1, both)
    numer_ref[...] += placed[:, :WIDTH]
    den_ref[...] += placed[:, WIDTH:]

    loads[5].wait()
    sib_tok_copy.wait_recv()
    tok_t[:, :ROWS] = mm(perm[...], tok[core], NT).astype(BF)
    tok_t[:, ROWS:] = mm(perm[...], sib_tok[...], NT).astype(BF)

    for copy in kz_copies:
        copy.wait_recv()
    keys23 = kv23[:, :, :WIDTH].reshape(WIDTH, WIDTH)
    values23 = kv23[:, :, WIDTH:].reshape(WIDTH, WIDTH)
    small_row = lax.rem(iota((8 * HEADS, WIDTH), 0), 8)
    wide_key = lax.rem(iota((8 * HEADS, WIDTH), 1), 48) >= 32
    mask23 = jnp.where(wide_key, small_row, small_row + 8)
    mask23 = (mask23 == 4) | ((mask23 >= 8) & (mask23 < 12))
    weights, both = level_forward(q_block23, keys23, values23, own23, mask23)
    w23[...] = weights
    placed = place(put23, both)
    numer = numer_ref[...] + placed[:, :WIDTH]
    den = den_ref[...] + placed[:, WIDTH:]
    attended = (numer / den).astype(BF)
    att_buf[0] = attended
    att_copy = push(att_buf.at[0], att_buf.at[1], sib_s.at[2], sib_r.at[2], sibling)

    inverse = 1.0 / den
    products = grad_att.astype(F32) * attended.astype(F32)
    stat_lane = iota((1, 128), 1)
    stats = jnp.zeros((ROWS, 128), F32)
    inverses, deltas = [], []
    for h in range(HEADS):
        inv = inverse[:, 64 * h : 64 * h + 1]
        delta = jnp.sum(products[:, 64 * h : 64 * h + 64], axis=1, keepdims=True)
        inverses.append(inv)
        deltas.append(delta)
        stats = jnp.where(stat_lane == h, inv, stats)
        stats = jnp.where(stat_lane == 8 + h, delta, stats)
    stats = jnp.concatenate(halves(stats), 1)

    def picked_stats(pick, rows_per_head):
        rows = HEADS * rows_per_head
        got = mm(pick, stats)
        got = got[:, :128] + got[:, 128:]
        at = iota((rows, 128), 0) // rows_per_head
        lanes = iota((rows, 128), 1)
        inv = jnp.sum(jnp.where(lanes == at, got, 0.0), axis=1, keepdims=True)
        delta = jnp.sum(jnp.where(lanes == at + 8, got, 0.0), axis=1, keepdims=True)
        return inv, delta

    inv, delta = picked_stats(pick23, 8)
    grad_q23, grad_kv = level_backward(
        w23[...], q_block23, g_block23, keys23, values23, inv, delta, own23
    )
    gsendz[...] = grad_kv.astype(BF).reshape(8, 48, 2 * WIDTH)
    rz_copies = [
        push(gsendz.at[d], grecvz.at[d], rz_s.at[d], rz_r.at[d], z_peer[d]) for d in range(1, 8)
    ]

    inv, delta = picked_stats(pick1, 64)
    grad_q1, grad_kv = level_backward(
        w1[...], q_block1, g_block1, keys1, values1, inv, delta, own1
    )
    gsend1[...] = grad_kv.astype(BF).reshape(4, 64, 2 * WIDTH)
    r1_copies = [
        push(gsend1.at[d], grecv1.at[d], r1_s.at[d], r1_r.at[d], group_peer[d])
        for d in range(1, 4)
    ]
    gq_acc[...] = place(put1, grad_q1) + place(put23, grad_q23)

    def level0_backward(p):
        queries, keys, values = pair(0, p), pair(WIDTH, p), pair(2 * WIDTH, p)
        grads = gatt[:, 128 * p : 128 * p + 128]
        parts = []
        for e in range(2):
            h = 2 * p + e
            probs = w0[h] * inverses[h]
            grad_probs = mm(grads * side[e], values, NT)
            grad_scores = (probs * (grad_probs - deltas[h])).astype(BF)
            parts.append((
                mm(grad_scores, keys) * SCALE,
                mm(grad_scores, queries, TN),
                mm(probs.astype(BF), grads, TN),
            ))
        merged = [jnp.where(low_lanes, a, b) for a, b in zip(*parts)]
        cols = slice(128 * p, 128 * p + 128)
        gq_acc[:, cols] += merged[0]
        gkv_acc[:, cols] = merged[1]
        gkv_acc[:, WIDTH + 128 * p : WIDTH + 128 * p + 128] = merged[2]

    level0_backward(0)
    level0_backward(1)

    total = gsendz[0].astype(F32)
    for d in range(1, 8):
        rz_copies[d - 1].wait_recv()
        total = total + grecvz[d].astype(F32)
    gsends[...] = mm(comp[...], total.astype(BF), TN).astype(BF).reshape(16, 16, 2 * WIDTH)
    rs_copies = [
        push(gsends.at[d], grecvs.at[d], rs_s.at[d], rs_r.at[d], group_peer[d])
        for d in range(1, 16)
    ]

    level0_backward(2)
    grad_q = gq_acc[...].astype(BF)
    gbuf[0, 0] = grad_q
    gq_copy = push(gbuf.at[0, 0], gbuf.at[0, 1], sib_s.at[3], sib_r.at[3], sibling)

    sib_gout_copy.wait_recv()
    gout_t[:, :ROWS] = mm(perm[...], gout[core], NT).astype(BF)
    gout_t[:, ROWS:] = mm(perm[...], sib_gout[...], NT).astype(BF)

    def weight_terms(r, p, left, own, other):
        term = mm(left[:, :ROWS], own) + mm(left[:, ROWS:], other)
        ysend[r, :, p] = term.astype(BF).reshape(4, 192, WIDTH)

    def y_stage(r):
        copies = []
        for d in range(1, 4):
            block = lax.rem(lax.div(y_peer[d], 2), 4)
            copies.append(push(
                ysend.at[r, block], yrecv.at[r, d], y_s.at[r, d], y_r.at[r, d], y_peer[d]
            ))
        return copies

    def z_stage(r, copies):
        for copy in copies:
            copy.wait_recv()
        total = ysend[r, y_at].astype(F32)
        for d in range(1, 4):
            total = total + yrecv[r, d].astype(F32)
        for n in range(8):
            rows = slice(24 * n, 24 * n + 24)
            zsend[r, n] = jnp.concatenate([total[0, rows], total[1, rows]], 0).astype(BF)
        out = []
        for d in range(1, 8):
            block = lax.rem(lax.div(z_peer[d], 8), 8)
            out.append(push(
                zsend.at[r, block], zrecv.at[r, d], z_s.at[r, d], z_r.at[r, d], z_peer[d]
            ))
        return out

    def x_stage(r, copies):
        total = zsend[r, z_at].astype(F32)
        for d in range(1, 8):
            copies[d - 1].wait_recv()
            total = total + zrecv[r, d].astype(F32)
        xbuf[r] = total
        out = []
        for n, d in enumerate((1, 8, 9)):
            out.append(push(xbuf.at[r], xrecv.at[r, n], x_s.at[r, n], x_r.at[r, n], group_peer[d]))
        return out

    att_copy.wait_recv()
    weight_terms(0, 0, gout_t, att_buf[0], att_buf[1])
    gq_copy.wait_recv()
    weight_terms(0, 1, tok_t, gbuf[0, 0], gbuf[0, 1])
    y0 = y_stage(0)

    def tiled(x):
        return jnp.concatenate([x] * HEADS, 0)

    total = gsend1[0].astype(F32)
    for d in range(1, 4):
        r1_copies[d - 1].wait_recv()
        total = total + grecv1[d].astype(F32)
    both1 = jnp.concatenate([own1, own1], 1)
    grad_kv = gkv_acc[...] + place(put1, jnp.where(both1, tiled(total), 0.0))
    total = gsends[0].astype(F32)
    for d in range(1, 16):
        rs_copies[d - 1].wait_recv()
        total = total + grecvs[d].astype(F32)
    both23 = jnp.concatenate([own23, own23], 1)
    grad_kv = grad_kv + place(put23, jnp.where(both23, tiled(total[:8]), 0.0))
    grad_kv = grad_kv.astype(BF)
    gbuf[1, 0] = grad_kv[:, :WIDTH]
    gbuf[2, 0] = grad_kv[:, WIDTH:]
    gk_copy = push(gbuf.at[1, 0], gbuf.at[1, 1], sib_s.at[4], sib_r.at[4], sibling)
    gv_copy = push(gbuf.at[2, 0], gbuf.at[2, 1], sib_s.at[5], sib_r.at[5], sibling)

    gk_copy.wait_recv()
    weight_terms(1, 0, tok_t, gbuf[1, 0], gbuf[1, 1])
    gv_copy.wait_recv()
    weight_terms(1, 1, tok_t, gbuf[2, 0], gbuf[2, 1])
    y1 = y_stage(1)

    def token_part(which):
        rows = pl.ds(pl.multiple_of(which * HALF, HALF), HALF)
        out = mm(gbuf[0, 0], wqkv[0, rows, :], NT)
        out = out + mm(gbuf[1, 0], wqkv[1, rows, :], NT)
        return out + mm(gbuf[2, 0], wqkv[2, rows, :], NT)

    def mixed_part(which):
        return mm(att_buf[0], wout[:, pl.ds(pl.multiple_of(which * HALF, HALF), HALF)])

    gtok_out[...] = token_part(other_head).astype(BF)
    gtok_copy = push(gtok_out, gtok_in, head_s.at[2], head_r.at[2], seq, other_head)
    z0 = z_stage(0, y0)
    mixed_out[...] = mixed_part(other_head).astype(BF)
    mixed_copy = push(mixed_out, mixed_in, head_s.at[3], head_r.at[3], seq, other_head)
    own_tokens = token_part(head)
    z1 = z_stage(1, y1)
    x0 = x_stage(0, z0)
    gtok_copy.wait_recv()
    gtok_ref[...] = (own_tokens + gtok_in[...].astype(F32)).astype(BF)
    own_mixed = mixed_part(head)
    mixed_copy.wait_recv()
    mixed_ref[...] = (own_mixed + mixed_in[...].astype(F32)).astype(BF)
    x1 = x_stage(1, z1)

    def finish(r, copies):
        for copy in copies:
            copy.wait_recv()
        straight = xbuf[r] + xrecv[r, 1]
        crossed = xrecv[r, 0] + xrecv[r, 2]
        total = jnp.where(core == x_at, straight, crossed)
        return [
            jnp.where(core == 0, total[24 * n : 24 * n + 12], total[24 * n + 12 : 24 * n + 24])
            for n in range(2)
        ]

    first, second = finish(0, x0)
    gwout_ref[...] = first
    gqkv_ref[0] = second
    first, second = finish(1, x1)
    gqkv_ref[1] = first
    gqkv_ref[2] = second
    for copy in sent:
        copy.wait_send()


def constants():
    at = np.arange(HALF)
    y, z, i = at // 192, at % 192 // 24, at % 24
    perm = np.zeros((HALF, HALF), np.float32)
    perm[at, z * 96 + y * 24 + i] = 1
    comp = np.zeros((48, 256), np.float32)
    for r in range(32):
        comp[r, r // 4 * 16 + r % 4] = 1
    for d in range(16):
        comp[32 + d, 16 * d + 4] = 1
    return jnp.asarray(perm, BF), jnp.asarray(comp, BF)


def per_device(tokens, w_qkv, w_out, grad_out, offsets):
    perm, comp = constants()
    vm = pltpu.VMEM
    dma = pltpu.SemaphoreType.DMA
    scratch = [
        vm((2, ROWS, HALF), BF), vm((2, ROWS, HALF), BF), vm((3, 2 * HALF, WIDTH), BF),
        vm((WIDTH, 2 * HALF), BF), vm((HALF, HALF), BF), vm((48, 256), BF),
        vm((ROWS, HALF), BF), vm((ROWS, HALF), BF),
        vm((ROWS, 3 * WIDTH), F32), vm((ROWS, 3 * WIDTH), BF),
        vm((4, 64, 2 * WIDTH), BF), vm((16, 16, 2 * WIDTH), BF), vm((8, 48, 2 * WIDTH), BF),
        vm((HEADS, ROWS, ROWS), F32), vm((WIDTH, ROWS), F32), vm((8 * HEADS, WIDTH), F32),
        vm((ROWS, WIDTH), F32), vm((ROWS, WIDTH), F32), vm((ROWS, WIDTH), BF),
        vm((2, ROWS, WIDTH), BF), vm((ROWS, WIDTH), F32), vm((ROWS, 2 * WIDTH), F32),
        vm((HALF, 2 * ROWS), BF), vm((HALF, 2 * ROWS), BF), vm((3, 2, ROWS, WIDTH), BF),
        vm((4, 64, 2 * WIDTH), BF), vm((4, 64, 2 * WIDTH), BF),
        vm((8, 48, 2 * WIDTH), BF), vm((8, 48, 2 * WIDTH), BF),
        vm((16, 16, 2 * WIDTH), BF), vm((16, 16, 2 * WIDTH), BF),
        vm((ROWS, HALF), BF), vm((ROWS, HALF), BF), vm((ROWS, HALF), BF), vm((ROWS, HALF), BF),
        vm((2, 4, 2, 192, WIDTH), BF), vm((2, 4, 2, 192, WIDTH), BF),
        vm((2, 8, 48, WIDTH), BF), vm((2, 8, 48, WIDTH), BF),
        vm((2, 48, WIDTH), F32), vm((2, 3, 48, WIDTH), F32),
        dma((6,)), dma((4,)), dma((4,)), dma((6,)), dma((6,)), dma((4,)), dma((4,)),
        dma((16,)), dma((16,)), dma((8,)), dma((8,)), dma((4,)), dma((4,)), dma((8,)), dma((8,)),
        dma((16,)), dma((16,)), dma((2, 4)), dma((2, 4)), dma((2, 8)), dma((2, 8)),
        dma((2, 3)), dma((2, 3)),
    ]
    anywhere = pl.BlockSpec(memory_space=pl.ANY)
    inside = pl.BlockSpec(memory_space=pltpu.VMEM)
    mixed, grad_tokens, grad_qkv, grad_w_out = pl.pallas_call(
        kernel,
        out_shape=(
            jax.ShapeDtypeStruct((ROWS, HALF), BF),
            jax.ShapeDtypeStruct((ROWS, HALF), BF),
            jax.ShapeDtypeStruct((3, 12, WIDTH), F32),
            jax.ShapeDtypeStruct((12, WIDTH), F32),
        ),
        in_specs=[anywhere] * 6 + [pl.BlockSpec(memory_space=pltpu.SMEM)],
        out_specs=(inside,) * 4,
        scratch_shapes=scratch,
        compiler_params=pltpu.CompilerParams(
            collective_id=0, has_side_effects=True, vmem_limit_bytes=56 * 2**20
        ),
        cost_estimate=pl.CostEstimate(
            flops=8 * 10**9, bytes_accessed=12 * 2**20, transcendentals=600000
        ),
    )(tokens, grad_out, jnp.transpose(w_qkv, (1, 0, 2)), w_out, perm, comp, offsets)
    return mixed, grad_tokens, jnp.transpose(grad_qkv, (1, 0, 2)), jnp.transpose(grad_w_out)


def solution(mesh):
    placed = (
        P("seq", "head"),
        P(None, None, "head"),
        P("head", None),
        P("seq", "head"),
        P(None, "head"),
    )
    return jax.shard_map(
        per_device,
        mesh=mesh,
        in_specs=placed,
        out_specs=(P("seq", "head"), P("seq", "head"), P("seq", None, "head"), P("head", "seq")),
        check_vma=False,
    )
```

```python
import jax
import jax.numpy as jnp
import numpy as np
from jax import lax
from jax.experimental import pallas as pl
from jax.experimental.pallas import tpu as pltpu
from jax.sharding import PartitionSpec as P

MESH = pl.DeviceIdType.MESH
BF = jnp.bfloat16
F32 = jnp.float32
ROWS = 256
WIDTH = 384
HALF = 768
HEADS = 6
SCALE = 0.125

NN = (((1,), (0,)), ((), ()))
NT = (((1,), (1,)), ((), ()))
TN = (((0,), (0,)), ((), ()))


def mm(a, b, dims=NN):
    return lax.dot_general(a, b, dims, preferred_element_type=F32)


def iota(shape, dim):
    return lax.broadcasted_iota(jnp.int32, shape, dim)


def halves(x):
    high = x.astype(BF)
    return high, (x - high.astype(F32)).astype(BF)


def place(spread, x):
    high, low = halves(x)
    return mm(spread, high) + mm(spread, low)


def by_head(pieces):
    lanes = iota((1, pieces[0].shape[1]), 1)
    lanes = jnp.where(lanes >= WIDTH, lanes - WIDTH, lanes)
    out = pieces[0]
    for h in range(1, HEADS):
        out = jnp.where(lanes >= 64 * h, pieces[h], out)
    return out


def block_mask(rows_per_head):
    rows = HEADS * rows_per_head
    head = iota((rows, WIDTH), 0) // rows_per_head
    return head == iota((rows, WIDTH), 1) // 64


def level_forward(q_block, keys, values, own_lanes, mask):
    weights = jnp.exp(mm(q_block, keys, NT))
    if mask is not None:
        weights = jnp.where(mask, weights, 0.0)
    total = jnp.sum(weights, axis=1, keepdims=True)
    numer = mm(weights.astype(BF), values)
    both = jnp.concatenate(
        [jnp.where(own_lanes, numer, 0.0), jnp.where(own_lanes, total, 0.0)], 1
    )
    return weights, both


def level_backward(weights, q_block, grad_block, keys, values, inverse, delta, own_lanes):
    probs = weights * inverse
    grad_probs = mm(grad_block, values, NT)
    grad_scores = (probs * (grad_probs - delta)).astype(BF)
    grad_values = mm(probs.astype(BF), grad_block, TN)
    grad_keys = mm(grad_scores, q_block, TN)
    grad_q = jnp.where(own_lanes, mm(grad_scores, keys) * SCALE, 0.0)
    return grad_q, jnp.concatenate([grad_keys, grad_values], 1)


def kernel(
    tok_hbm, gout_hbm, wqkv_hbm, wout_hbm, perm_hbm, comp_hbm, off_ref,
    mixed_ref, gtok_ref, gqkv_ref, gwout_ref,
    tok, gout, wqkv, wout, perm, comp, sib_tok, sib_gout,
    acc, qkv, kv1, sv, sv_in, kvz, kvh, w0, w1, w23, numer_ref, den_ref, gatt, att_buf,
    gq_acc, gkv_acc, tok_t, gout_t, gbuf, gsend1, grecv1, gs, gs_in, gx, gx_in, gz, gz_in,
    gf, gf_in, mixed_out, mixed_in, gtok_out, gtok_in, part_a,
    ysend, yrecv, ysend_a, yrecv_a, ysend_b, yrecv_b, zsend, zrecv, zsend_a, zrecv_a,
    zsend_b, zrecv_b, xbuf, xrecv,
    local_sem, head_s, head_r, sib_s, sib_r, k1_s, k1_r, kz_s, kz_r, kx_s, kx_r,
    r1_s, r1_r, rx_s, rx_r, rz_s, rz_r, y_s, y_r, z_s, z_r, x_s, x_r,
):
    seq = lax.axis_index("seq")
    head = lax.axis_index("head")

    def bit(step):
        return lax.rem(lax.div(seq, step), 2)

    core = bit(1)
    y_at = lax.rem(lax.div(seq, 2), 4)
    z_at = lax.rem(lax.div(seq, 8), 8)
    x_at = lax.div(seq, 64)

    def flipped(d, steps):
        other = seq
        for b, step in enumerate(steps):
            if d >> b & 1:
                other = other + (1 - 2 * bit(step)) * step
        return other

    z_peer = [flipped(d, (8, 16, 32)) for d in range(8)]
    chip_peer = [flipped(d, (2, 4, 64)) for d in range(8)]
    pair_peer = [flipped(d, (1, 2)) for d in range(4)]
    cross_peer = [flipped(d, (1, 64)) for d in range(4)]
    sibling = pair_peer[1]
    other_head = 1 - head

    def push(src, dst, send, recv, to_seq, to_head=None):
        target = (to_seq, head if to_head is None else to_head)
        copy = pltpu.make_async_remote_copy(
            src_ref=src, dst_ref=dst, send_sem=send, recv_sem=recv,
            device_id=target, device_id_type=MESH,
        )
        copy.start()
        sent.append(copy)
        return copy

    sent = []

    loads = []
    for n, (src, dst) in enumerate([
        (tok_hbm, tok.at[head]), (wqkv_hbm, wqkv), (gout_hbm, gout.at[head]),
        (wout_hbm, wout), (comp_hbm, comp), (perm_hbm, perm),
    ]):
        copy = pltpu.make_async_copy(src, dst, local_sem.at[n])
        copy.start()
        loads.append(copy)

    barrier = pltpu.get_barrier_semaphore()
    peers = [(seq, other_head)]
    peers += [(sibling, head), (pair_peer[3], head), (cross_peer[3], head)]
    peers += [(chip_peer[d], head) for d in range(1, 8)]
    peers += [(z_peer[d], head) for d in range(1, 8)]
    for peer in peers:
        pl.semaphore_signal(barrier, inc=1, device_id=peer, device_id_type=MESH)
    pl.semaphore_wait(barrier, len(peers))

    tok_copy = push(tok_hbm, tok.at[head], head_s.at[0], head_r.at[0], seq, other_head)

    loads[0].wait()
    loads[1].wait()
    for j in range(3):
        cols = slice(WIDTH * j, WIDTH * (j + 1))
        acc[:, cols] = mm(tok[head], wqkv[j, pl.ds(pl.multiple_of(head * HALF, HALF), HALF), :])

    lane = iota((64, ROWS), 1)
    row = iota((64, ROWS), 0)
    pick1 = jnp.concatenate(
        [jnp.where(lane == 4 * row + off_ref[1, h], 1.0, 0.0) for h in range(HEADS)], 0
    ).astype(BF)
    lane8 = iota((8, ROWS), 1)
    row8 = iota((8, ROWS), 0)

    def spot(at, h):
        return jnp.where(
            at < 4, 64 * at + off_ref[2, h], jnp.where(at == 4, off_ref[3, h], -1)
        )

    pick23 = jnp.concatenate(
        [jnp.where(lane8 == spot(row8, h), 1.0, 0.0) for h in range(HEADS)], 0
    ).astype(BF)
    at1 = iota((1, WIDTH), 1)
    spot1 = 4 * at1 + off_ref[1, 0]
    for h in range(1, HEADS):
        spot1 = jnp.where(at1 >= 64 * h, 4 * (at1 - 64 * h) + off_ref[1, h], spot1)
    put1 = jnp.where(iota((ROWS, WIDTH), 0) == spot1, 1.0, 0.0).astype(BF)
    at23 = iota((1, 8 * HEADS), 1)
    spot23 = spot(at23, 0)
    for h in range(1, HEADS):
        spot23 = jnp.where(at23 >= 8 * h, spot(at23 - 8 * h, h), spot23)
    put23 = jnp.where(iota((ROWS, 8 * HEADS), 0) == spot23, 1.0, 0.0).astype(BF)
    own1 = block_mask(64)
    own23 = block_mask(8)

    tok_copy.wait_recv()
    gout_copy = push(gout_hbm, gout.at[head], head_s.at[1], head_r.at[1], seq, other_head)
    for j in range(3):
        cols = slice(WIDTH * j, WIDTH * (j + 1))
        other_rows = pl.ds(pl.multiple_of(other_head * HALF, HALF), HALF)
        part = acc[:, cols] + mm(tok[other_head], wqkv[j, other_rows, :])
        if j == 0:
            part = part.astype(BF).astype(F32) * SCALE
        qkv[:, cols] = part.astype(BF)

    key_value = qkv[:, WIDTH:]
    picked23 = mm(pick23, key_value)
    small = by_head([picked23[8 * h : 8 * h + 8] for h in range(HEADS)])
    sv[0] = small[:, :WIDTH]
    sv[1] = small[:, WIDTH:]
    sv_copy = push(sv.at[1 - core], sv_in, sib_s.at[0], sib_r.at[0], sibling)
    picked1 = mm(pick1, key_value)
    kv1[0] = by_head([picked1[64 * h : 64 * h + 64] for h in range(HEADS)]).astype(BF)
    first = core == 0
    sv_copy.wait_recv()
    mine, theirs = sv[core], sv_in[...]
    kvz[0] = jnp.concatenate(
        [jnp.where(first, mine, theirs), jnp.where(first, theirs, mine)], 0
    ).astype(BF)
    kz_copies = [
        push(kvz.at[0], kvz.at[d], kz_s.at[d], kz_r.at[d], z_peer[d]) for d in range(1, 8)
    ]
    k1_copies = [
        push(kv1.at[0], kv1.at[d], k1_s.at[d], k1_r.at[d], pair_peer[d]) for d in range(1, 4)
    ]
    sib_tok_copy = push(tok.at[1 - core], sib_tok, sib_s.at[1], sib_r.at[1], sibling)

    q_block1 = jnp.where(own1, mm(pick1, qkv[:, :WIDTH]), 0.0).astype(BF)
    q_block23 = jnp.where(own23, mm(pick23, qkv[:, :WIDTH]), 0.0).astype(BF)

    low_lanes = iota((1, 128), 1) < 64
    side = [jnp.where(low_lanes, 1.0, 0.0).astype(BF), jnp.where(low_lanes, 0.0, 1.0).astype(BF)]

    def pair(start, p):
        return qkv[:, start + 128 * p : start + 128 * p + 128]

    def level0_forward(p):
        queries, keys, values = pair(0, p), pair(WIDTH, p), pair(2 * WIDTH, p)
        parts = []
        for e in range(2):
            weights = jnp.exp(mm(queries * side[e], keys, NT))
            w0[2 * p + e] = weights
            parts.append((mm(weights.astype(BF), values), jnp.sum(weights, axis=1, keepdims=True)))
        numer_ref[:, 128 * p : 128 * p + 128] = jnp.where(low_lanes, parts[0][0], parts[1][0])
        den_ref[:, 128 * p : 128 * p + 128] = jnp.where(low_lanes, parts[0][1], parts[1][1])

    level0_forward(0)

    loads[4].wait()
    for copy in kz_copies:
        copy.wait_recv()
    kvh[core, 0:80] = mm(comp[...], kvz[...].reshape(128, WIDTH)).astype(BF)
    kx_copies = []
    for d in range(1, 8):
        if d < 4:
            src, dst = kvh.at[core, 0:80], kvh.at[core, 80 * d : 80 * d + 80]
        else:
            src, dst = kvh.at[core, 64:80], kvh.at[core, 256 + 16 * d : 272 + 16 * d]
        kx_copies.append(push(src, dst, kx_s.at[d], kx_r.at[d], chip_peer[d]))

    level0_forward(1)
    for copy in kx_copies:
        copy.wait_recv()
    kvh_copy = push(kvh.at[core], kvh.at[core], sib_s.at[2], sib_r.at[2], sibling)
    level0_forward(2)

    loads[2].wait()
    loads[3].wait()
    gout_copy.wait_recv()
    sib_gout_copy = push(gout.at[1 - core], sib_gout, sib_s.at[3], sib_r.at[3], sibling)
    grad_att = (mm(gout[0], wout[:, :HALF], NT) + mm(gout[1], wout[:, HALF:], NT)).astype(BF)
    gatt[...] = grad_att
    g_block1 = jnp.where(own1, mm(pick1, grad_att), 0.0).astype(BF)
    g_block23 = jnp.where(own23, mm(pick23, grad_att), 0.0).astype(BF)

    for copy in k1_copies:
        copy.wait_recv()
    keys1, values1 = kv1[:, :, :WIDTH].reshape(256, WIDTH), kv1[:, :, WIDTH:].reshape(256, WIDTH)
    weights, both = level_forward(q_block1, keys1, values1, own1, None)
    w1[...] = weights
    placed = place(put1, both)
    numer_ref[...] += placed[:, :WIDTH]
    den_ref[...] += placed[:, WIDTH:]

    loads[5].wait()
    sib_gout_copy.wait_recv()
    gout_t[:, :ROWS] = mm(perm[...], gout[core], NT).astype(BF)
    gout_t[:, ROWS:] = mm(perm[...], sib_gout[...], NT).astype(BF)
    sib_tok_copy.wait_recv()
    tok_t[:, :ROWS] = mm(perm[...], tok[core], NT).astype(BF)
    tok_t[:, ROWS:] = mm(perm[...], sib_tok[...], NT).astype(BF)

    kvh_copy.wait_recv()
    keys23, values23 = kvh[0], kvh[1]
    small_row = lax.rem(iota((8 * HEADS, WIDTH), 0), 8)
    key_at = iota((8 * HEADS, WIDTH), 1)
    wide_key = (key_at >= 320) | (lax.rem(key_at, 80) >= 64)
    mask23 = jnp.where(wide_key, small_row, small_row + 8)
    mask23 = (mask23 == 4) | ((mask23 >= 8) & (mask23 < 12))
    weights, both = level_forward(q_block23, keys23, values23, own23, mask23)
    w23[...] = weights
    placed = place(put23, both)
    numer = numer_ref[...] + placed[:, :WIDTH]
    den = den_ref[...] + placed[:, WIDTH:]
    attended = (numer / den).astype(BF)
    att_buf[0] = attended
    att_copy = push(att_buf.at[0], att_buf.at[1], sib_s.at[4], sib_r.at[4], sibling)

    inverse = 1.0 / den
    products = grad_att.astype(F32) * attended.astype(F32)
    stat_lane = iota((1, 128), 1)
    stats = jnp.zeros((ROWS, 128), F32)
    inverses, deltas = [], []
    for h in range(HEADS):
        inv = inverse[:, 64 * h : 64 * h + 1]
        delta = jnp.sum(products[:, 64 * h : 64 * h + 64], axis=1, keepdims=True)
        inverses.append(inv)
        deltas.append(delta)
        stats = jnp.where(stat_lane == h, inv, stats)
        stats = jnp.where(stat_lane == 8 + h, delta, stats)
    stats = jnp.concatenate(halves(stats), 1)

    def picked_stats(pick, rows_per_head):
        rows = HEADS * rows_per_head
        got = mm(pick, stats)
        got = got[:, :128] + got[:, 128:]
        at = iota((rows, 128), 0) // rows_per_head
        lanes = iota((rows, 128), 1)
        inv = jnp.sum(jnp.where(lanes == at, got, 0.0), axis=1, keepdims=True)
        delta = jnp.sum(jnp.where(lanes == at + 8, got, 0.0), axis=1, keepdims=True)
        return inv, delta

    inv, delta = picked_stats(pick23, 8)
    grad_q23, grad_kv = level_backward(
        w23[...], q_block23, g_block23, keys23, values23, inv, delta, own23
    )
    grad_kv = grad_kv.astype(BF)
    gs[0] = grad_kv[:, :WIDTH]
    gs[1] = grad_kv[:, WIDTH:]
    gs_copy = push(gs.at[1 - core], gs_in, sib_s.at[5], sib_r.at[5], sibling)

    def out_cols(which):
        return pl.ds(pl.multiple_of(which * HALF, HALF), HALF)

    mixed_out[...] = mm(attended, wout[:, out_cols(other_head)]).astype(BF)
    mixed_copy = push(mixed_out, mixed_in, head_s.at[3], head_r.at[3], seq, other_head)
    inv, delta = picked_stats(pick1, 64)
    grad_q1, grad_kv = level_backward(
        w1[...], q_block1, g_block1, keys1, values1, inv, delta, own1
    )
    gsend1[...] = grad_kv.astype(BF).reshape(4, 64, 2 * WIDTH)
    r1_copies = [
        push(gsend1.at[d], grecv1.at[d], r1_s.at[d], r1_r.at[d], pair_peer[d])
        for d in range(1, 4)
    ]
    gs_copy.wait_recv()
    gx[...] = (gs[core].astype(F32) + gs_in[...].astype(F32)).astype(BF)

    def back_rows(d):
        return slice(80 * d, 80 * d + 80) if d < 4 else slice(256 + 16 * d, 272 + 16 * d)

    rx_copies = [
        push(gx.at[back_rows(d)], gx_in.at[back_rows(d)], rx_s.at[d], rx_r.at[d], chip_peer[d])
        for d in range(1, 8)
    ]
    gq_acc[...] = place(put1, grad_q1) + place(put23, grad_q23)

    def weight_term(left, own, other, arrived):
        term = mm(left[:, :ROWS], own)
        arrived.wait_recv()
        return term + mm(left[:, ROWS:], other[...])

    def y_block(d):
        return lax.rem(lax.div(chip_peer[d], 2), 4)

    def y_send(n, source, landing):
        return [
            push(source.at[y_block(d)], landing.at[d], y_s.at[n, d], y_r.at[n, d], chip_peer[d])
            for d in range(1, 4)
        ]

    term = weight_term(gout_t, att_buf[0], att_buf.at[1], att_copy)
    ysend[0] = term.astype(BF).reshape(4, 192, WIDTH)
    yw = y_send(0, ysend.at[0], yrecv.at[0])

    def level0_backward(p):
        queries, keys, values = pair(0, p), pair(WIDTH, p), pair(2 * WIDTH, p)
        grads = gatt[:, 128 * p : 128 * p + 128]
        parts = []
        for e in range(2):
            h = 2 * p + e
            probs = w0[h] * inverses[h]
            grad_probs = mm(grads * side[e], values, NT)
            grad_scores = (probs * (grad_probs - deltas[h])).astype(BF)
            parts.append((
                mm(grad_scores, keys) * SCALE,
                mm(grad_scores, queries, TN),
                mm(probs.astype(BF), grads, TN),
            ))
        merged = [jnp.where(low_lanes, a, b) for a, b in zip(*parts)]
        cols = slice(128 * p, 128 * p + 128)
        gq_acc[:, cols] += merged[0]
        gkv_acc[:, cols] = merged[1]
        gkv_acc[:, WIDTH + 128 * p : WIDTH + 128 * p + 128] = merged[2]

    level0_backward(0)
    for copy in rx_copies:
        copy.wait_recv()
    total = gx[0:80].astype(F32)
    for d in range(1, 4):
        total = total + gx_in[back_rows(d)].astype(F32)
    wide = total[64:80]
    for d in range(4, 8):
        wide = wide + gx_in[back_rows(d)].astype(F32)
    total = jnp.concatenate([total[:64], wide], 0).astype(BF)
    gz[...] = mm(comp[...], total, TN).astype(BF).reshape(8, 16, WIDTH)
    rz_copies = [
        push(gz.at[d], gz_in.at[d], rz_s.at[d], rz_r.at[d], z_peer[d]) for d in range(1, 8)
    ]
    level0_backward(1)
    level0_backward(2)
    part_a[...] = mm(attended, wout[:, out_cols(head)])
    grad_q = gq_acc[...].astype(BF)
    gbuf[0, 0] = grad_q
    gq_copy = push(gbuf.at[0, 0], gbuf.at[0, 1], sib_s.at[6], sib_r.at[6], sibling)

    for copy in rz_copies:
        copy.wait_recv()
    total = gz[0].astype(F32)
    for d in range(1, 8):
        total = total + gz_in[d].astype(F32)
    gf[0] = total[:8]
    gf[1] = total[8:]
    gf_copy = push(gf.at[1 - core], gf_in, sib_s.at[7], sib_r.at[7], sibling)

    term = weight_term(tok_t, grad_q, gbuf.at[0, 1], gq_copy)
    ysend[1] = term.astype(BF).reshape(4, 192, WIDTH)
    yq = y_send(1, ysend.at[1], yrecv.at[1])

    def head_rows(which):
        return pl.ds(pl.multiple_of(which * HALF, HALF), HALF)

    def tiled(x):
        return jnp.concatenate([x] * HEADS, 0)

    total = gsend1[0].astype(F32)
    for d in range(1, 4):
        r1_copies[d - 1].wait_recv()
        total = total + grecv1[d].astype(F32)
    both1 = jnp.concatenate([own1, own1], 1)
    grad_kv = gkv_acc[...] + place(put1, jnp.where(both1, tiled(total), 0.0))
    gf_copy.wait_recv()
    mine, theirs = gf[core], gf_in[...]
    total = jnp.concatenate([jnp.where(first, mine, theirs), jnp.where(first, theirs, mine)], 1)
    both23 = jnp.concatenate([own23, own23], 1)
    grad_kv = grad_kv + place(put23, jnp.where(both23, tiled(total), 0.0))
    grad_kv = grad_kv.astype(BF)
    gbuf[1, 0] = grad_kv[:, :WIDTH]
    gbuf[2, 0] = grad_kv[:, WIDTH:]
    gk_copy = push(gbuf.at[1, 0], gbuf.at[1, 1], sib_s.at[8], sib_r.at[8], sibling)
    gv_copy = push(gbuf.at[2, 0], gbuf.at[2, 1], sib_s.at[9], sib_r.at[9], sibling)

    term_k = weight_term(tok_t, gbuf[1, 0], gbuf.at[1, 1], gk_copy).astype(BF)
    term_v = weight_term(tok_t, gbuf[2, 0], gbuf.at[2, 1], gv_copy).astype(BF)
    ysend_a[:, 0] = term_k[:, :256].reshape(4, 192, 256)
    ysend_a[:, 1] = term_v[:, :256].reshape(4, 192, 256)
    ya = y_send(2, ysend_a, yrecv_a)
    ysend_b[:, 0] = term_k[:, 256:].reshape(4, 192, 128)
    ysend_b[:, 1] = term_v[:, 256:].reshape(4, 192, 128)
    yb = y_send(3, ysend_b, yrecv_b)

    def token_part(which):
        out = mm(gbuf[0, 0], wqkv[0, head_rows(which), :], NT)
        out = out + mm(gbuf[1, 0], wqkv[1, head_rows(which), :], NT)
        return out + mm(gbuf[2, 0], wqkv[2, head_rows(which), :], NT)

    gtok_out[...] = token_part(other_head).astype(BF)
    gtok_copy = push(gtok_out, gtok_in, head_s.at[2], head_r.at[2], seq, other_head)

    def z_send(n, total, source, landing):
        for m in range(8):
            rows = slice(24 * m, 24 * m + 24)
            source[m] = jnp.concatenate([total[0][rows], total[1][rows]], 0).astype(BF)
        out = []
        for d in range(1, 8):
            block = lax.rem(lax.div(z_peer[d], 8), 8)
            out.append(
                push(source.at[block], landing.at[d], z_s.at[n, d], z_r.at[n, d], z_peer[d])
            )
        return out

    def y_total(own, landing):
        out = own.astype(F32)
        for d in range(1, 4):
            out = out + landing[d].astype(F32)
        return out

    def z_total(own, landing):
        out = own.astype(F32)
        for d in range(1, 8):
            out = out + landing[d].astype(F32)
        return out

    def arrive(copies):
        for copy in copies:
            copy.wait_recv()

    def x_send(r):
        return [
            push(xbuf.at[r], xrecv.at[r, d], x_s.at[r, d], x_r.at[r, d], cross_peer[d])
            for d in range(1, 4)
        ]

    arrive(yw)
    arrive(yq)
    totals = [y_total(ysend[p, y_at], yrecv.at[p]) for p in range(2)]
    z0 = z_send(0, totals, zsend, zrecv)
    arrive(ya)
    za = z_send(1, y_total(ysend_a[y_at], yrecv_a), zsend_a, zrecv_a)
    arrive(yb)
    zb = z_send(2, y_total(ysend_b[y_at], yrecv_b), zsend_b, zrecv_b)
    arrive(z0)
    xbuf[0] = z_total(zsend[z_at], zrecv)
    x0 = x_send(0)
    own_tokens = token_part(head)
    gtok_copy.wait_recv()
    gtok_ref[...] = (own_tokens + gtok_in[...].astype(F32)).astype(BF)
    mixed_copy.wait_recv()
    mixed_ref[...] = (part_a[...] + mixed_in[...].astype(F32)).astype(BF)
    arrive(za)
    xbuf[1, :, :256] = z_total(zsend_a[z_at], zrecv_a)
    arrive(zb)
    xbuf[1, :, 256:] = z_total(zsend_b[z_at], zrecv_b)
    x1 = x_send(1)

    def finish(r, copies):
        arrive(copies)
        straight = xbuf[r] + xrecv[r, 2]
        crossed = xrecv[r, 1] + xrecv[r, 3]
        total = jnp.where(core == x_at, straight, crossed)
        return [
            jnp.where(first, total[24 * n : 24 * n + 12], total[24 * n + 12 : 24 * n + 24])
            for n in range(2)
        ]

    one, two = finish(0, x0)
    gwout_ref[...] = one
    gqkv_ref[0] = two
    one, two = finish(1, x1)
    gqkv_ref[1] = one
    gqkv_ref[2] = two
    for copy in sent:
        copy.wait_send()


def finish_kernel(mixed, gtok, gqkv, gwout, mixed_out, gtok_out, gqkv_out, gwout_out):
    mixed_out[...] = mixed[...]
    gtok_out[...] = gtok[...]
    gwout_out[...] = gwout[...]
    for j in range(3):
        gqkv_out[:, j, :] = gqkv[j]


def constants():
    at = np.arange(HALF)
    y, z, i = at // 192, at % 192 // 24, at % 24
    perm = np.zeros((HALF, HALF), np.float32)
    perm[at, z * 96 + y * 24 + i] = 1
    comp = np.zeros((80, 128), np.float32)
    for d in range(8):
        for e in range(2):
            for i in range(4):
                comp[8 * d + 4 * e + i, 16 * d + 8 * e + i] = 1
            comp[64 + 2 * d + e, 16 * d + 8 * e + 4] = 1
    return jnp.asarray(perm, BF), jnp.asarray(comp, BF)


def per_device(tokens, w_qkv, w_out, grad_out, offsets):
    perm, comp = constants()
    vm = pltpu.VMEM
    dma = pltpu.SemaphoreType.DMA
    scratch = [
        vm((2, ROWS, HALF), BF), vm((2, ROWS, HALF), BF), vm((3, 2 * HALF, WIDTH), BF),
        vm((WIDTH, 2 * HALF), BF), vm((HALF, HALF), BF), vm((80, 128), BF),
        vm((ROWS, HALF), BF), vm((ROWS, HALF), BF),
        vm((ROWS, 3 * WIDTH), F32), vm((ROWS, 3 * WIDTH), BF), vm((4, 64, 2 * WIDTH), BF),
        vm((2, 8, WIDTH), F32), vm((8, WIDTH), F32), vm((8, 16, WIDTH), BF),
        vm((2, WIDTH, WIDTH), BF),
        vm((HEADS, ROWS, ROWS), F32), vm((WIDTH, ROWS), F32), vm((8 * HEADS, WIDTH), F32),
        vm((ROWS, WIDTH), F32), vm((ROWS, WIDTH), F32), vm((ROWS, WIDTH), BF),
        vm((2, ROWS, WIDTH), BF), vm((ROWS, WIDTH), F32), vm((ROWS, 2 * WIDTH), F32),
        vm((HALF, 2 * ROWS), BF), vm((HALF, 2 * ROWS), BF), vm((3, 2, ROWS, WIDTH), BF),
        vm((4, 64, 2 * WIDTH), BF), vm((4, 64, 2 * WIDTH), BF),
        vm((2, WIDTH, WIDTH), BF), vm((WIDTH, WIDTH), BF),
        vm((WIDTH, WIDTH), BF), vm((WIDTH, WIDTH), BF),
        vm((8, 16, WIDTH), BF), vm((8, 16, WIDTH), BF),
        vm((2, 8, WIDTH), F32), vm((8, WIDTH), F32),
        vm((ROWS, HALF), BF), vm((ROWS, HALF), BF), vm((ROWS, HALF), BF), vm((ROWS, HALF), BF),
        vm((ROWS, HALF), F32),
        vm((2, 4, 192, WIDTH), BF), vm((2, 4, 192, WIDTH), BF),
        vm((4, 2, 192, 256), BF), vm((4, 2, 192, 256), BF),
        vm((4, 2, 192, 128), BF), vm((4, 2, 192, 128), BF),
        vm((8, 48, WIDTH), BF), vm((8, 48, WIDTH), BF),
        vm((8, 48, 256), BF), vm((8, 48, 256), BF), vm((8, 48, 128), BF), vm((8, 48, 128), BF),
        vm((2, 48, WIDTH), F32), vm((2, 4, 48, WIDTH), F32),
        dma((6,)), dma((4,)), dma((4,)), dma((10,)), dma((10,)), dma((4,)), dma((4,)),
        dma((8,)), dma((8,)), dma((8,)), dma((8,)), dma((4,)), dma((4,)),
        dma((8,)), dma((8,)), dma((8,)), dma((8,)), dma((4, 4)), dma((4, 4)),
        dma((3, 8)), dma((3, 8)), dma((2, 4)), dma((2, 4)),
    ]
    anywhere = pl.BlockSpec(memory_space=pl.ANY)
    inside = pl.BlockSpec(memory_space=pltpu.VMEM)
    results = pl.pallas_call(
        kernel,
        out_shape=(
            jax.ShapeDtypeStruct((ROWS, HALF), BF),
            jax.ShapeDtypeStruct((ROWS, HALF), BF),
            jax.ShapeDtypeStruct((3, 12, WIDTH), F32),
            jax.ShapeDtypeStruct((12, WIDTH), F32),
        ),
        in_specs=[anywhere] * 6 + [pl.BlockSpec(memory_space=pltpu.SMEM)],
        out_specs=(inside,) * 4,
        scratch_shapes=scratch,
        compiler_params=pltpu.CompilerParams(
            collective_id=0, has_side_effects=True, vmem_limit_bytes=56 * 2**20
        ),
        cost_estimate=pl.CostEstimate(
            flops=8 * 10**9, bytes_accessed=12 * 2**20, transcendentals=600000
        ),
    )(tokens, grad_out, jnp.transpose(w_qkv, (1, 0, 2)), w_out, perm, comp, offsets)
    mixed, grad_tokens, grad_qkv, grad_w_out = pl.pallas_call(
        finish_kernel,
        out_shape=(
            jax.ShapeDtypeStruct((ROWS, HALF), BF),
            jax.ShapeDtypeStruct((ROWS, HALF), BF),
            jax.ShapeDtypeStruct((12, 3, WIDTH), F32),
            jax.ShapeDtypeStruct((12, WIDTH), F32),
        ),
        in_specs=[inside] * 4,
        out_specs=(inside,) * 4,
    )(*results)
    return mixed, grad_tokens, grad_qkv, jnp.transpose(grad_w_out)


def solution(mesh):
    placed = (
        P("seq", "head"),
        P(None, None, "head"),
        P("head", None),
        P("seq", "head"),
        P(None, "head"),
    )
    return jax.shard_map(
        per_device,
        mesh=mesh,
        in_specs=placed,
        out_specs=(P("seq", "head"), P("seq", "head"), P("seq", None, "head"), P("head", "seq")),
        check_vma=False,
    )
```

```python
import jax
import jax.numpy as jnp
import numpy as np
from jax import lax
from jax.experimental import pallas as pl
from jax.experimental.pallas import tpu as pltpu
from jax.sharding import PartitionSpec as P

MESH = pl.DeviceIdType.MESH
BF = jnp.bfloat16
F32 = jnp.float32
ROWS = 256
WIDTH = 384
HALF = 768
HEADS = 6
SCALE = 0.125
FAR_FIRST = (4, 5, 3, 6, 2, 7, 1)

NN = (((1,), (0,)), ((), ()))
NT = (((1,), (1,)), ((), ()))
TN = (((0,), (0,)), ((), ()))


def mm(a, b, dims=NN):
    return lax.dot_general(a, b, dims, preferred_element_type=F32)


def iota(shape, dim):
    return lax.broadcasted_iota(jnp.int32, shape, dim)


def halves(x):
    high = x.astype(BF)
    return high, (x - high.astype(F32)).astype(BF)


def place(spread, x):
    high, low = halves(x)
    return mm(spread, high) + mm(spread, low)


def by_head(pieces):
    lanes = iota((1, pieces[0].shape[1]), 1)
    lanes = jnp.where(lanes >= WIDTH, lanes - WIDTH, lanes)
    out = pieces[0]
    for h in range(1, HEADS):
        out = jnp.where(lanes >= 64 * h, pieces[h], out)
    return out


def block_mask(rows_per_head):
    rows = HEADS * rows_per_head
    head = iota((rows, WIDTH), 0) // rows_per_head
    return head == iota((rows, WIDTH), 1) // 64


def level_forward(q_block, keys, values, own_lanes, mask):
    weights = jnp.exp(mm(q_block, keys, NT))
    if mask is not None:
        weights = jnp.where(mask, weights, 0.0)
    total = jnp.sum(weights, axis=1, keepdims=True)
    numer = mm(weights.astype(BF), values)
    both = jnp.concatenate(
        [jnp.where(own_lanes, numer, 0.0), jnp.where(own_lanes, total, 0.0)], 1
    )
    return weights, both


def level_backward(weights, q_block, grad_block, keys, values, inverse, delta, own_lanes):
    probs = weights * inverse
    grad_probs = mm(grad_block, values, NT)
    grad_scores = (probs * (grad_probs - delta)).astype(BF)
    grad_values = mm(probs.astype(BF), grad_block, TN)
    grad_keys = mm(grad_scores, q_block, TN)
    grad_q = jnp.where(own_lanes, mm(grad_scores, keys) * SCALE, 0.0)
    return grad_q, jnp.concatenate([grad_keys, grad_values], 1)


def kernel(
    tok_hbm, gout_hbm, wqkv_hbm, wout_hbm, perm_hbm, comp_hbm, off_ref,
    mixed_ref, gtok_ref, gqkv_ref, gwout_ref,
    tok, gout, wqkv, wout, perm, comp, sib_tok, sib_gout,
    acc, qkv, kv1, sv, sv_in, kvz, kvh, w0, w1, w23, numer_ref, den_ref, gatt, att_buf,
    gq_acc, gkv_acc, tok_t, gout_t, gbuf, gsend1, grecv1, gs, gs_in, gx, gx_in, gz, gz_in,
    gf, gf_in, picks, rows_out, rows_in, xin, fbuf, mixed_out, mixed_in, gtok_out, gtok_in, part_a,
    ysend, yrecv, ysend_a, yrecv_a, ysend_b, yrecv_b, zsend, zrecv, zsend_a, zrecv_a,
    zsend_b, zrecv_b, xbuf, xrecv,
    local_sem, head_s, head_r, sib_s, sib_r, k1_s, k1_r, kz_s, kz_r, kx_s, kx_r,
    r1_s, r1_r, rx_s, rx_r, rz_s, rz_r, y_s, y_r, z_s, z_r, x_s, x_r, w_s, w_r,
):
    seq = lax.axis_index("seq")
    head = lax.axis_index("head")

    def bit(step):
        return lax.rem(lax.div(seq, step), 2)

    core = bit(1)
    y_at = lax.rem(lax.div(seq, 2), 4)
    z_at = lax.rem(lax.div(seq, 8), 8)
    x_at = lax.div(seq, 64)

    def flipped(d, steps):
        other = seq
        for b, step in enumerate(steps):
            if d >> b & 1:
                other = other + (1 - 2 * bit(step)) * step
        return other

    z_peer = [flipped(d, (8, 16, 32)) for d in range(8)]
    chip_peer = [flipped(d, (2, 4, 64)) for d in range(8)]
    pair_peer = [flipped(d, (1, 2)) for d in range(4)]
    cross_peer = [flipped(d, (1, 64)) for d in range(4)]
    sibling = pair_peer[1]
    other_head = 1 - head

    def made(src, dst, send, recv, to_seq, to_head=None):
        target = (to_seq, head if to_head is None else to_head)
        return pltpu.make_async_remote_copy(
            src_ref=src, dst_ref=dst, send_sem=send, recv_sem=recv,
            device_id=target, device_id_type=MESH,
        )

    def push(*copy_args):
        copy = made(*copy_args)
        copy.start()
        sent.append(copy)
        return copy

    sent = []

    loads = []
    for n, (src, dst) in enumerate([
        (tok_hbm, tok.at[head]), (wqkv_hbm, wqkv), (gout_hbm, gout.at[head]),
        (wout_hbm, wout), (comp_hbm, comp), (perm_hbm, perm),
    ]):
        copy = pltpu.make_async_copy(src, dst, local_sem.at[n])
        copy.start()
        loads.append(copy)

    lane = iota((64, ROWS), 1)
    row = iota((64, ROWS), 0)
    pick1 = jnp.concatenate(
        [jnp.where(lane == 4 * row + off_ref[1, h], 1.0, 0.0) for h in range(HEADS)], 0
    ).astype(BF)
    lane8 = iota((8, ROWS), 1)
    row8 = iota((8, ROWS), 0)

    def spot(at, h):
        return jnp.where(
            at < 4, 64 * at + off_ref[2, h], jnp.where(at == 4, off_ref[3, h], -1)
        )

    pick23 = jnp.concatenate(
        [jnp.where(lane8 == spot(row8, h), 1.0, 0.0) for h in range(HEADS)], 0
    ).astype(BF)
    at1 = iota((1, WIDTH), 1)
    spot1 = 4 * at1 + off_ref[1, 0]
    for h in range(1, HEADS):
        spot1 = jnp.where(at1 >= 64 * h, 4 * (at1 - 64 * h) + off_ref[1, h], spot1)
    put1 = jnp.where(iota((ROWS, WIDTH), 0) == spot1, 1.0, 0.0).astype(BF)
    at23 = iota((1, 8 * HEADS), 1)
    spot23 = spot(at23, 0)
    for h in range(1, HEADS):
        spot23 = jnp.where(at23 >= 8 * h, spot(at23 - 8 * h, h), spot23)
    put23 = jnp.where(iota((ROWS, 8 * HEADS), 0) == spot23, 1.0, 0.0).astype(BF)
    own1 = block_mask(64)
    own23 = block_mask(8)

    picks[0] = pick23
    barrier = pltpu.get_barrier_semaphore()
    peers = [(seq, other_head)]
    peers += [(sibling, head), (pair_peer[3], head), (cross_peer[3], head)]
    peers += [(chip_peer[d], head) for d in range(1, 8)]
    peers += [(z_peer[d], head) for d in range(1, 8)]
    for peer in peers:
        pl.semaphore_signal(barrier, inc=1, device_id=peer, device_id_type=MESH)
    pl.semaphore_wait(barrier, len(peers))

    picks_copy = push(picks.at[0], picks.at[1], head_s.at[4], head_r.at[4], seq, other_head)

    loads[0].wait()
    chosen_own = mm(pick23, tok[head]).astype(BF)
    picks_copy.wait_recv()
    rows_out[...] = mm(picks[1], tok[head]).astype(BF)
    rows_copy = push(rows_out, rows_in, head_s.at[5], head_r.at[5], seq, other_head)
    tok_copy = push(tok_hbm, tok.at[head], head_s.at[0], head_r.at[0], seq, other_head)

    def gout_push(n, rows):
        return push(
            gout_hbm.at[rows], gout.at[head, rows], head_s.at[n], head_r.at[n], seq, other_head
        )

    gout_copies = [gout_push(1, slice(0, 112))]
    loads[1].wait()

    def head_rows(which):
        return pl.ds(pl.multiple_of(which * HALF, HALF), HALF)

    small_own = [mm(chosen_own, wqkv[j, head_rows(head), :]) for j in (1, 2)]
    rows_copy.wait_recv()
    chosen_other = rows_in[...]
    for j in (1, 2):
        part = small_own[j - 1] + mm(chosen_other, wqkv[j, head_rows(other_head), :])
        part = by_head([part[8 * h : 8 * h + 8] for h in range(HEADS)])
        sv[j - 1] = part.astype(BF).astype(F32)
    sv_copy = push(sv.at[1 - core], sv_in, sib_s.at[0], sib_r.at[0], sibling)

    for j in range(3):
        cols = slice(WIDTH * j, WIDTH * (j + 1))
        acc[:, cols] = mm(tok[head], wqkv[j, pl.ds(pl.multiple_of(head * HALF, HALF), HALF), :])

    first = core == 0
    sv_copy.wait_recv()
    mine, theirs = sv[core], sv_in[...]
    kvz[0] = jnp.concatenate(
        [jnp.where(first, mine, theirs), jnp.where(first, theirs, mine)], 0
    ).astype(BF)
    kz_copies = [
        push(kvz.at[0], kvz.at[d], kz_s.at[d], kz_r.at[d], z_peer[d]) for d in FAR_FIRST
    ]
    loads[4].wait()
    for copy in kz_copies:
        copy.wait_recv()
    kvh[core, 0:80] = mm(comp[...], kvz[...].reshape(128, WIDTH)).astype(BF)
    kx_copies = []
    for d in (6, 5, 7, 4, 2, 1, 3):
        if d < 4:
            src, dst = kvh.at[core, 0:80], kvh.at[core, 80 * d : 80 * d + 80]
        else:
            src, dst = kvh.at[core, 64:80], kvh.at[core, 256 + 16 * d : 272 + 16 * d]
        kx_copies.append(push(src, dst, kx_s.at[d], kx_r.at[d], chip_peer[d]))
    gout_copies.append(gout_push(6, slice(112, ROWS)))

    tok_copy.wait_recv()
    for j in range(3):
        cols = slice(WIDTH * j, WIDTH * (j + 1))
        other_rows = pl.ds(pl.multiple_of(other_head * HALF, HALF), HALF)
        part = acc[:, cols] + mm(tok[other_head], wqkv[j, other_rows, :])
        if j == 0:
            part = part.astype(BF).astype(F32) * SCALE
        qkv[:, cols] = part.astype(BF)

    key_value = qkv[:, WIDTH:]
    picked1 = mm(pick1, key_value)
    kv1[0] = by_head([picked1[64 * h : 64 * h + 64] for h in range(HEADS)]).astype(BF)
    k1_copies = [
        push(kv1.at[0], kv1.at[d], k1_s.at[d], k1_r.at[d], pair_peer[d]) for d in range(1, 3)
    ]
    sib_tok_copy = push(tok.at[1 - core], sib_tok, sib_s.at[1], sib_r.at[1], sibling)

    q_block1 = jnp.where(own1, mm(pick1, qkv[:, :WIDTH]), 0.0).astype(BF)
    q_block23 = jnp.where(own23, mm(pick23, qkv[:, :WIDTH]), 0.0).astype(BF)

    low_lanes = iota((1, 128), 1) < 64
    side = [jnp.where(low_lanes, 1.0, 0.0).astype(BF), jnp.where(low_lanes, 0.0, 1.0).astype(BF)]

    def pair(start, p):
        return qkv[:, start + 128 * p : start + 128 * p + 128]

    def level0_forward(p):
        queries, keys, values = pair(0, p), pair(WIDTH, p), pair(2 * WIDTH, p)
        parts = []
        for e in range(2):
            weights = jnp.exp(mm(queries * side[e], keys, NT))
            w0[2 * p + e] = weights
            parts.append((mm(weights.astype(BF), values), jnp.sum(weights, axis=1, keepdims=True)))
        numer_ref[:, 128 * p : 128 * p + 128] = jnp.where(low_lanes, parts[0][0], parts[1][0])
        den_ref[:, 128 * p : 128 * p + 128] = jnp.where(low_lanes, parts[0][1], parts[1][1])

    level0_forward(0)

    level0_forward(1)
    for copy in kx_copies:
        copy.wait_recv()
    kvh_copy = push(kvh.at[core], kvh.at[core], sib_s.at[2], sib_r.at[2], sibling)
    level0_forward(2)

    k1_copies[1].wait_recv()
    k1_copies.append(push(kv1.at[2], kv1.at[3], k1_s.at[3], k1_r.at[3], sibling))
    k1_copies[0].wait_recv()
    k1_copies[2].wait_recv()
    keys1, values1 = kv1[:, :, :WIDTH].reshape(256, WIDTH), kv1[:, :, WIDTH:].reshape(256, WIDTH)
    weights, both = level_forward(q_block1, keys1, values1, own1, None)
    w1[...] = weights
    placed = place(put1, both)
    numer_ref[...] += placed[:, :WIDTH]
    den_ref[...] += placed[:, WIDTH:]

    loads[5].wait()
    sib_tok_copy.wait_recv()
    tok_t[:, :ROWS] = mm(perm[...], tok[core], NT).astype(BF)
    tok_t[:, ROWS:] = mm(perm[...], sib_tok[...], NT).astype(BF)

    loads[2].wait()
    loads[3].wait()
    for copy in gout_copies:
        copy.wait_recv()
    sib_gout_copy = push(gout.at[1 - core], sib_gout, sib_s.at[3], sib_r.at[3], sibling)
    grad_att = (mm(gout[0], wout[:, :HALF], NT) + mm(gout[1], wout[:, HALF:], NT)).astype(BF)
    gatt[...] = grad_att
    g_block1 = jnp.where(own1, mm(pick1, grad_att), 0.0).astype(BF)
    g_block23 = jnp.where(own23, mm(pick23, grad_att), 0.0).astype(BF)

    kvh_copy.wait_recv()
    keys23, values23 = kvh[0], kvh[1]
    small_row = lax.rem(iota((8 * HEADS, WIDTH), 0), 8)
    key_at = iota((8 * HEADS, WIDTH), 1)
    wide_key = (key_at >= 320) | (lax.rem(key_at, 80) >= 64)
    mask23 = jnp.where(wide_key, small_row, small_row + 8)
    mask23 = (mask23 == 4) | ((mask23 >= 8) & (mask23 < 12))
    weights, both = level_forward(q_block23, keys23, values23, own23, mask23)
    w23[...] = weights
    placed = place(put23, both)
    numer = numer_ref[...] + placed[:, :WIDTH]
    den = den_ref[...] + placed[:, WIDTH:]
    attended = (numer / den).astype(BF)
    att_buf[0] = attended
    att_copy = push(att_buf.at[0], att_buf.at[1], sib_s.at[4], sib_r.at[4], sibling)

    inverse = 1.0 / den
    products = grad_att.astype(F32) * attended.astype(F32)
    stat_lane = iota((1, 128), 1)
    stats = jnp.zeros((ROWS, 128), F32)
    inverses, deltas = [], []
    for h in range(HEADS):
        inv = inverse[:, 64 * h : 64 * h + 1]
        delta = jnp.sum(products[:, 64 * h : 64 * h + 64], axis=1, keepdims=True)
        inverses.append(inv)
        deltas.append(delta)
        stats = jnp.where(stat_lane == h, inv, stats)
        stats = jnp.where(stat_lane == 8 + h, delta, stats)
    stats = jnp.concatenate(halves(stats), 1)

    def picked_stats(pick, rows_per_head):
        rows = HEADS * rows_per_head
        got = mm(pick, stats)
        got = got[:, :128] + got[:, 128:]
        at = iota((rows, 128), 0) // rows_per_head
        lanes = iota((rows, 128), 1)
        inv = jnp.sum(jnp.where(lanes == at, got, 0.0), axis=1, keepdims=True)
        delta = jnp.sum(jnp.where(lanes == at + 8, got, 0.0), axis=1, keepdims=True)
        return inv, delta

    inv, delta = picked_stats(pick23, 8)
    grad_q23, grad_kv = level_backward(
        w23[...], q_block23, g_block23, keys23, values23, inv, delta, own23
    )
    grad_kv = grad_kv.astype(BF)
    gs[0] = grad_kv[:, :WIDTH]
    gs[1] = grad_kv[:, WIDTH:]
    gs_copy = push(gs.at[1 - core], gs_in, sib_s.at[5], sib_r.at[5], sibling)

    def out_cols(which):
        return pl.ds(pl.multiple_of(which * HALF, HALF), HALF)

    inv, delta = picked_stats(pick1, 64)
    grad_q1, grad_kv = level_backward(
        w1[...], q_block1, g_block1, keys1, values1, inv, delta, own1
    )
    gsend1[...] = grad_kv.astype(BF).reshape(4, 64, 2 * WIDTH)
    r1_copies = [
        push(gsend1.at[d], grecv1.at[d], r1_s.at[d], r1_r.at[d], sibling) for d in (1, 3)
    ]
    def level0_backward(p):
        queries, keys, values = pair(0, p), pair(WIDTH, p), pair(2 * WIDTH, p)
        grads = gatt[:, 128 * p : 128 * p + 128]
        parts = []
        for e in range(2):
            h = 2 * p + e
            probs = w0[h] * inverses[h]
            grad_probs = mm(grads * side[e], values, NT)
            grad_scores = (probs * (grad_probs - deltas[h])).astype(BF)
            parts.append((
                mm(grad_scores, keys) * SCALE,
                mm(grad_scores, queries, TN),
                mm(probs.astype(BF), grads, TN),
            ))
        merged = [jnp.where(low_lanes, a, b) for a, b in zip(*parts)]
        cols = slice(128 * p, 128 * p + 128)
        gq_acc[:, cols] += merged[0]
        gkv_acc[:, cols] = merged[1]
        gkv_acc[:, WIDTH + 128 * p : WIDTH + 128 * p + 128] = merged[2]

    gq_acc[...] = place(put1, grad_q1) + place(put23, grad_q23)
    level0_backward(0)
    gs_copy.wait_recv()
    gx[...] = (gs[core].astype(F32) + gs_in[...].astype(F32)).astype(BF)

    def back_rows(d):
        return slice(80 * d, 80 * d + 80) if d < 4 else slice(256 + 16 * d, 272 + 16 * d)

    rx_copies = [
        push(gx.at[back_rows(d)], gx_in.at[back_rows(d)], rx_s.at[d], rx_r.at[d], chip_peer[d])
        for d in range(1, 8)
    ]
    def weight_term(left, own, other, arrived):
        term = mm(left[:, :ROWS], own)
        arrived.wait_recv()
        return term + mm(left[:, ROWS:], other[...])

    def y_block(d):
        return lax.rem(lax.div(chip_peer[d], 2), 4)

    def y_made(n, source, landing):
        return [
            made(source.at[y_block(d)], landing.at[d], y_s.at[n, d], y_r.at[n, d], chip_peer[d])
            for d in range(1, 4)
        ]

    def begin(copies):
        for copy in copies:
            copy.start()

    def y_send(n, source, landing):
        copies = y_made(n, source, landing)
        begin(copies)
        sent.extend(copies)
        return copies

    def y_total(own, landing):
        out = own.astype(F32)
        for d in range(1, 4):
            out = out + landing[d].astype(F32)
        return out

    def z_total(own, landing):
        out = own.astype(F32)
        for d in range(1, 8):
            out = out + landing[d].astype(F32)
        return out

    def arrive(copies):
        for copy in copies:
            copy.wait_recv()

    reducer = core == x_at
    x_copies = [
        made(ysend.at[n], xin.at[n], w_s.at[n], w_r.at[n], cross_peer[2]) for n in range(2)
    ]
    y_early = [y_made(n, ysend.at[n], yrecv.at[n]) for n in range(2)]

    def x_first(n, term):
        ysend[n] = term.astype(BF).reshape(4, 192, WIDTH)

        @pl.when(jnp.logical_not(reducer))
        def _():
            x_copies[n].start()

    def y_after_x(n):
        @pl.when(reducer)
        def _():
            x_copies[n].wait_recv()
            ysend[n] = (ysend[n].astype(F32) + xin[n].astype(F32)).astype(BF)
            begin(y_early[n])

    sib_gout_copy.wait_recv()
    gout_t[:, :ROWS] = mm(perm[...], gout[core], NT).astype(BF)
    gout_t[:, ROWS:] = mm(perm[...], sib_gout[...], NT).astype(BF)
    x_first(0, weight_term(gout_t, att_buf[0], att_buf.at[1], att_copy))

    level0_backward(1)
    level0_backward(2)
    part_a[...] = mm(attended, wout[:, out_cols(head)])
    grad_q = gq_acc[...].astype(BF)
    gbuf[0, 0] = grad_q
    gq_copy = push(gbuf.at[0, 0], gbuf.at[0, 1], sib_s.at[6], sib_r.at[6], sibling)

    for copy in rx_copies:
        copy.wait_recv()
    total = gx[0:80].astype(F32)
    for d in range(1, 4):
        total = total + gx_in[back_rows(d)].astype(F32)
    wide = total[64:80]
    for d in range(4, 8):
        wide = wide + gx_in[back_rows(d)].astype(F32)
    total = jnp.concatenate([total[:64], wide], 0).astype(BF)
    gz[...] = mm(comp[...], total, TN).astype(BF).reshape(8, 16, WIDTH)
    rz_copies = [
        push(gz.at[d], gz_in.at[d], rz_s.at[d], rz_r.at[d], z_peer[d]) for d in FAR_FIRST
    ]
    x_first(1, weight_term(tok_t, grad_q, gbuf.at[0, 1], gq_copy))
    mixed_out[...] = mm(attended, wout[:, out_cols(other_head)]).astype(BF)
    mixed_copy = push(mixed_out, mixed_in, head_s.at[3], head_r.at[3], seq, other_head)
    y_after_x(0)
    arrive(r1_copies)
    gsend1[2] = (gsend1[2].astype(F32) + grecv1[3].astype(F32)).astype(BF)
    r1_copies.append(push(gsend1.at[2], grecv1.at[2], r1_s.at[2], r1_r.at[2], pair_peer[2]))
    for copy in rz_copies:
        copy.wait_recv()
    total = gz[0].astype(F32)
    for d in range(1, 8):
        total = total + gz_in[d].astype(F32)
    gf[0] = total[:8]
    gf[1] = total[8:]
    gf_copy = push(gf.at[1 - core], gf_in, sib_s.at[7], sib_r.at[7], sibling)

    def tiled(x):
        return jnp.concatenate([x] * HEADS, 0)

    total = gsend1[0].astype(F32)
    r1_copies[2].wait_recv()
    for d in range(1, 3):
        total = total + grecv1[d].astype(F32)
    both1 = jnp.concatenate([own1, own1], 1)
    grad_kv = gkv_acc[...] + place(put1, jnp.where(both1, tiled(total), 0.0))
    gf_copy.wait_recv()
    mine, theirs = gf[core], gf_in[...]
    total = jnp.concatenate([jnp.where(first, mine, theirs), jnp.where(first, theirs, mine)], 1)
    both23 = jnp.concatenate([own23, own23], 1)
    grad_kv = grad_kv + place(put23, jnp.where(both23, tiled(total), 0.0))
    grad_kv = grad_kv.astype(BF)
    gbuf[1, 0] = grad_kv[:, :WIDTH]
    gbuf[2, 0] = grad_kv[:, WIDTH:]
    gk_copy = push(gbuf.at[1, 0], gbuf.at[1, 1], sib_s.at[8], sib_r.at[8], sibling)
    gv_copy = push(gbuf.at[2, 0], gbuf.at[2, 1], sib_s.at[9], sib_r.at[9], sibling)

    term_k = weight_term(tok_t, gbuf[1, 0], gbuf.at[1, 1], gk_copy)
    term_v = weight_term(tok_t, gbuf[2, 0], gbuf.at[2, 1], gv_copy)
    ysend_a[:, 0] = term_k[:, :256].astype(BF).reshape(4, 192, 256)
    ysend_a[:, 1] = term_v[:, :256].astype(BF).reshape(4, 192, 256)
    ya = y_send(2, ysend_a, yrecv_a)

    def z_made(n, source, landing):
        out = []
        for d in FAR_FIRST:
            block = lax.rem(lax.div(z_peer[d], 8), 8)
            out.append(made(source.at[block], landing.at[d], z_s.at[n, d], z_r.at[n, d], z_peer[d]))
        return out

    def z_send(n, source, landing):
        copies = z_made(n, source, landing)
        begin(copies)
        sent.extend(copies)
        return copies

    def z_blocks(pieces, m):
        return jnp.concatenate([piece[24 * m : 24 * m + 24] for piece in pieces], 0).astype(BF)

    quarters = [term[192 * n : 192 * n + 192, 256:] for term in (term_k, term_v) for n in range(4)]
    for m in range(8):
        zsend_b[m] = z_blocks(quarters, m)
    zb = z_send(2, zsend_b, zrecv_b)

    y_after_x(1)
    def token_part(which):
        out = mm(gbuf[0, 0], wqkv[0, head_rows(which), :], NT)
        out = out + mm(gbuf[1, 0], wqkv[1, head_rows(which), :], NT)
        return out + mm(gbuf[2, 0], wqkv[2, head_rows(which), :], NT)

    gtok_out[...] = token_part(other_head).astype(BF)
    gtok_copy = push(gtok_out, gtok_in, head_s.at[2], head_r.at[2], seq, other_head)

    own_tokens = token_part(head)
    arrive(ya)
    totals = y_total(ysend_a[y_at], yrecv_a)
    for m in range(8):
        zsend_a[m] = z_blocks([totals[0], totals[1]], m)
    za = z_send(1, zsend_a, zrecv_a)
    z_early = z_made(0, zsend, zrecv)
    f_copy = made(fbuf.at[0], fbuf.at[1], sib_s.at[10], sib_r.at[10], sibling)

    @pl.when(reducer)
    def _():
        arrive(y_early[0])
        arrive(y_early[1])
        totals = [y_total(ysend[p, y_at], yrecv.at[p]) for p in range(2)]
        for m in range(8):
            zsend[m] = z_blocks(totals, m)
        begin(z_early)

    arrive(zb)
    totals = z_total(zsend_b[z_at], zrecv_b)
    for n in range(4):
        ysend_b[n] = jnp.concatenate(
            [totals[24 * n : 24 * n + 24], totals[96 + 24 * n : 120 + 24 * n]], 0
        ).astype(BF)
    yb = y_send(3, ysend_b, yrecv_b)
    @pl.when(reducer)
    def _():
        arrive(z_early)
        fbuf[0] = z_total(zsend[z_at], zrecv)
        f_copy.start()

    gtok_copy.wait_recv()
    gtok_ref[...] = (own_tokens + gtok_in[...].astype(F32)).astype(BF)
    mixed_copy.wait_recv()
    mixed_ref[...] = (part_a[...] + mixed_in[...].astype(F32)).astype(BF)
    arrive(yb)
    xbuf[:, 256:] = y_total(ysend_b[y_at], yrecv_b)
    arrive(za)
    xbuf[:, :256] = z_total(zsend_a[z_at], zrecv_a)
    x1 = [
        push(xbuf, xrecv.at[d], x_s.at[d], x_r.at[d], cross_peer[d]) for d in range(1, 4)
    ]

    def finish(total):
        return [
            jnp.where(first, total[24 * n : 24 * n + 12], total[24 * n + 12 : 24 * n + 24])
            for n in range(2)
        ]

    @pl.when(jnp.logical_not(reducer))
    def _():
        f_copy.wait_recv()
        fbuf[0] = fbuf[1]

    one, two = finish(fbuf[0])
    gwout_ref[...] = one
    gqkv_ref[0] = two
    arrive(x1)
    straight = xbuf[...] + xrecv[2]
    crossed = xrecv[1] + xrecv[3]
    one, two = finish(jnp.where(reducer, straight, crossed))
    gqkv_ref[1] = one
    gqkv_ref[2] = two
    for copy in sent:
        copy.wait_send()

    @pl.when(reducer)
    def _():
        for copy in y_early[0] + y_early[1] + z_early + [f_copy]:
            copy.wait_send()

    @pl.when(jnp.logical_not(reducer))
    def _():
        for copy in x_copies:
            copy.wait_send()


def finish_kernel(mixed, gtok, gqkv, gwout, mixed_out, gtok_out, gqkv_out, gwout_out):
    mixed_out[...] = mixed[...]
    gtok_out[...] = gtok[...]
    gwout_out[...] = gwout[...]
    for j in range(3):
        gqkv_out[:, j, :] = gqkv[j]


def constants():
    at = np.arange(HALF)
    y, z, i = at // 192, at % 192 // 24, at % 24
    perm = np.zeros((HALF, HALF), np.float32)
    perm[at, z * 96 + y * 24 + i] = 1
    comp = np.zeros((80, 128), np.float32)
    for d in range(8):
        for e in range(2):
            for i in range(4):
                comp[8 * d + 4 * e + i, 16 * d + 8 * e + i] = 1
            comp[64 + 2 * d + e, 16 * d + 8 * e + 4] = 1
    return jnp.asarray(perm, BF), jnp.asarray(comp, BF)


def per_device(tokens, w_qkv, w_out, grad_out, offsets):
    perm, comp = constants()
    vm = pltpu.VMEM
    dma = pltpu.SemaphoreType.DMA
    scratch = [
        vm((2, ROWS, HALF), BF), vm((2, ROWS, HALF), BF), vm((3, 2 * HALF, WIDTH), BF),
        vm((WIDTH, 2 * HALF), BF), vm((HALF, HALF), BF), vm((80, 128), BF),
        vm((ROWS, HALF), BF), vm((ROWS, HALF), BF),
        vm((ROWS, 3 * WIDTH), F32), vm((ROWS, 3 * WIDTH), BF), vm((4, 64, 2 * WIDTH), BF),
        vm((2, 8, WIDTH), F32), vm((8, WIDTH), F32), vm((8, 16, WIDTH), BF),
        vm((2, WIDTH, WIDTH), BF),
        vm((HEADS, ROWS, ROWS), F32), vm((WIDTH, ROWS), F32), vm((8 * HEADS, WIDTH), F32),
        vm((ROWS, WIDTH), F32), vm((ROWS, WIDTH), F32), vm((ROWS, WIDTH), BF),
        vm((2, ROWS, WIDTH), BF), vm((ROWS, WIDTH), F32), vm((ROWS, 2 * WIDTH), F32),
        vm((HALF, 2 * ROWS), BF), vm((HALF, 2 * ROWS), BF), vm((3, 2, ROWS, WIDTH), BF),
        vm((4, 64, 2 * WIDTH), BF), vm((4, 64, 2 * WIDTH), BF),
        vm((2, WIDTH, WIDTH), BF), vm((WIDTH, WIDTH), BF),
        vm((WIDTH, WIDTH), BF), vm((WIDTH, WIDTH), BF),
        vm((8, 16, WIDTH), BF), vm((8, 16, WIDTH), BF),
        vm((2, 8, WIDTH), F32), vm((8, WIDTH), F32), vm((2, 48, ROWS), BF),
        vm((48, HALF), BF), vm((48, HALF), BF), vm((2, 4, 192, WIDTH), BF), vm((2, 48, WIDTH), F32),
        vm((ROWS, HALF), BF), vm((ROWS, HALF), BF), vm((ROWS, HALF), BF), vm((ROWS, HALF), BF),
        vm((ROWS, HALF), F32),
        vm((2, 4, 192, WIDTH), BF), vm((2, 4, 192, WIDTH), BF),
        vm((4, 2, 192, 256), BF), vm((4, 2, 192, 256), BF),
        vm((4, 48, 128), BF), vm((4, 48, 128), BF),
        vm((8, 48, WIDTH), BF), vm((8, 48, WIDTH), BF),
        vm((8, 48, 256), BF), vm((8, 48, 256), BF), vm((8, 192, 128), BF), vm((8, 192, 128), BF),
        vm((48, WIDTH), F32), vm((4, 48, WIDTH), F32),
        dma((6,)), dma((7,)), dma((7,)), dma((11,)), dma((11,)), dma((4,)), dma((4,)),
        dma((8,)), dma((8,)), dma((8,)), dma((8,)), dma((4,)), dma((4,)),
        dma((8,)), dma((8,)), dma((8,)), dma((8,)), dma((4, 4)), dma((4, 4)),
        dma((3, 8)), dma((3, 8)), dma((4,)), dma((4,)), dma((2,)), dma((2,)),
    ]
    anywhere = pl.BlockSpec(memory_space=pl.ANY)
    inside = pl.BlockSpec(memory_space=pltpu.VMEM)
    results = pl.pallas_call(
        kernel,
        out_shape=(
            jax.ShapeDtypeStruct((ROWS, HALF), BF),
            jax.ShapeDtypeStruct((ROWS, HALF), BF),
            jax.ShapeDtypeStruct((3, 12, WIDTH), F32),
            jax.ShapeDtypeStruct((12, WIDTH), F32),
        ),
        in_specs=[anywhere] * 6 + [pl.BlockSpec(memory_space=pltpu.SMEM)],
        out_specs=(inside,) * 4,
        scratch_shapes=scratch,
        compiler_params=pltpu.CompilerParams(
            collective_id=0, has_side_effects=True, vmem_limit_bytes=56 * 2**20
        ),
        cost_estimate=pl.CostEstimate(
            flops=8 * 10**9, bytes_accessed=12 * 2**20, transcendentals=600000
        ),
    )(tokens, grad_out, jnp.transpose(w_qkv, (1, 0, 2)), w_out, perm, comp, offsets)
    mixed, grad_tokens, grad_qkv, grad_w_out = pl.pallas_call(
        finish_kernel,
        out_shape=(
            jax.ShapeDtypeStruct((ROWS, HALF), BF),
            jax.ShapeDtypeStruct((ROWS, HALF), BF),
            jax.ShapeDtypeStruct((12, 3, WIDTH), F32),
            jax.ShapeDtypeStruct((12, WIDTH), F32),
        ),
        in_specs=[inside] * 4,
        out_specs=(inside,) * 4,
    )(*results)
    return mixed, grad_tokens, grad_qkv, jnp.transpose(grad_w_out)


def solution(mesh):
    placed = (
        P("seq", "head"),
        P(None, None, "head"),
        P("head", None),
        P("seq", "head"),
        P(None, "head"),
    )
    return jax.shard_map(
        per_device,
        mesh=mesh,
        in_specs=placed,
        out_specs=(P("seq", "head"), P("seq", "head"), P("seq", None, "head"), P("head", "seq")),
        check_vma=False,
    )
```

```python
import jax
import jax.numpy as jnp
import numpy as np
from jax import lax
from jax.experimental import pallas as pl
from jax.experimental.pallas import tpu as pltpu
from jax.sharding import PartitionSpec as P

MESH = pl.DeviceIdType.MESH
BF = jnp.bfloat16
F32 = jnp.float32
ROWS = 256
WIDTH = 384
HALF = 768
HEADS = 6
SCALE = 0.125
FAR_FIRST = (4, 5, 3, 6, 2, 7, 1)

NN = (((1,), (0,)), ((), ()))
NT = (((1,), (1,)), ((), ()))
TN = (((0,), (0,)), ((), ()))


def mm(a, b, dims=NN):
    return lax.dot_general(a, b, dims, preferred_element_type=F32)


def iota(shape, dim):
    return lax.broadcasted_iota(jnp.int32, shape, dim)


def halves(x):
    high = x.astype(BF)
    return high, (x - high.astype(F32)).astype(BF)


def place(spread, x):
    high, low = halves(x)
    return mm(spread, high) + mm(spread, low)


def by_head(pieces):
    lanes = iota((1, pieces[0].shape[1]), 1)
    lanes = jnp.where(lanes >= WIDTH, lanes - WIDTH, lanes)
    out = pieces[0]
    for h in range(1, HEADS):
        out = jnp.where(lanes >= 64 * h, pieces[h], out)
    return out


def block_mask(rows_per_head):
    rows = HEADS * rows_per_head
    head = iota((rows, WIDTH), 0) // rows_per_head
    return head == iota((rows, WIDTH), 1) // 64


def level_forward(q_block, keys, values, own_lanes, mask):
    weights = jnp.exp(mm(q_block, keys, NT))
    if mask is not None:
        weights = jnp.where(mask, weights, 0.0)
    total = jnp.sum(weights, axis=1, keepdims=True)
    numer = mm(weights.astype(BF), values)
    both = jnp.concatenate(
        [jnp.where(own_lanes, numer, 0.0), jnp.where(own_lanes, total, 0.0)], 1
    )
    return weights, both


def level_backward(weights, q_block, grad_block, keys, values, total, delta, own_lanes):
    probs = weights / total
    grad_probs = mm(grad_block, values, NT)
    grad_scores = (probs * (grad_probs - delta)).astype(BF)
    grad_values = mm(probs.astype(BF), grad_block, TN)
    grad_keys = mm(grad_scores, q_block, TN)
    grad_q = jnp.where(own_lanes, mm(grad_scores, keys) * SCALE, 0.0)
    return grad_q, jnp.concatenate([grad_keys, grad_values], 1)


def kernel(
    tok_hbm, gout_hbm, wqkv_hbm, wout_hbm, perm_hbm, comp_hbm, off_ref,
    mixed_ref, gtok_ref, gqkv_ref, gwout_ref,
    tok, gout, wqkv, wout, perm, comp, sib_tok, sib_gout,
    acc, qkv, kv1, sv, sv_in, kvz, kvh, w0, w1, w23, numer_ref, den_ref, gatt, att_buf,
    gq_acc, gkv_acc, tok_t, gout_t, gbuf, gsend1, grecv1, gs, gs_in, gx, gx_in, gz, gz_in,
    gf, gf_in, picks, rows_out, rows_in, xin, fbuf, mixed_out, mixed_in, gtok_out, gtok_in, part_a,
    ysend, yrecv, ysend_a, yrecv_a, ysend_b, yrecv_b, zsend, zrecv, zsend_a, zrecv_a,
    zsend_b, zrecv_b, xbuf, xrecv,
    local_sem, head_s, head_r, sib_s, sib_r, k1_s, k1_r, kz_s, kz_r, kx_s, kx_r,
    r1_s, r1_r, rx_s, rx_r, rz_s, rz_r, y_s, y_r, z_s, z_r, x_s, x_r, w_s, w_r,
):
    seq = lax.axis_index("seq")
    head = lax.axis_index("head")

    def bit(step):
        return lax.rem(lax.div(seq, step), 2)

    core = bit(1)
    y_at = lax.rem(lax.div(seq, 2), 4)
    z_at = lax.rem(lax.div(seq, 8), 8)
    x_at = lax.div(seq, 64)

    def flipped(d, steps):
        other = seq
        for b, step in enumerate(steps):
            if d >> b & 1:
                other = other + (1 - 2 * bit(step)) * step
        return other

    z_peer = [flipped(d, (8, 16, 32)) for d in range(8)]
    chip_peer = [flipped(d, (2, 4, 64)) for d in range(8)]
    pair_peer = [flipped(d, (1, 2)) for d in range(4)]
    cross_peer = [flipped(d, (1, 64)) for d in range(4)]
    sibling = pair_peer[1]
    other_head = 1 - head

    def made(src, dst, send, recv, to_seq, to_head=None):
        target = (to_seq, head if to_head is None else to_head)
        return pltpu.make_async_remote_copy(
            src_ref=src, dst_ref=dst, send_sem=send, recv_sem=recv,
            device_id=target, device_id_type=MESH,
        )

    def push(*copy_args):
        copy = made(*copy_args)
        copy.start()
        sent.append(copy)
        return copy

    sent = []

    loads = []
    for n, (src, dst) in enumerate([
        (tok_hbm, tok.at[head]), (wqkv_hbm, wqkv), (gout_hbm, gout.at[head]),
        (wout_hbm, wout), (comp_hbm, comp), (perm_hbm, perm),
    ]):
        copy = pltpu.make_async_copy(src, dst, local_sem.at[n])
        copy.start()
        loads.append(copy)

    lane = iota((64, ROWS), 1)
    row = iota((64, ROWS), 0)
    pick1 = jnp.concatenate(
        [jnp.where(lane == 4 * row + off_ref[1, h], 1.0, 0.0) for h in range(HEADS)], 0
    ).astype(BF)
    lane8 = iota((8, ROWS), 1)
    row8 = iota((8, ROWS), 0)

    def spot(at, h):
        return jnp.where(
            at < 4, 64 * at + off_ref[2, h], jnp.where(at == 4, off_ref[3, h], -1)
        )

    pick23 = jnp.concatenate(
        [jnp.where(lane8 == spot(row8, h), 1.0, 0.0) for h in range(HEADS)], 0
    ).astype(BF)
    at1 = iota((1, WIDTH), 1)
    spot1 = 4 * at1 + off_ref[1, 0]
    for h in range(1, HEADS):
        spot1 = jnp.where(at1 >= 64 * h, 4 * (at1 - 64 * h) + off_ref[1, h], spot1)
    put1 = jnp.where(iota((ROWS, WIDTH), 0) == spot1, 1.0, 0.0).astype(BF)
    at23 = iota((1, 8 * HEADS), 1)
    spot23 = spot(at23, 0)
    for h in range(1, HEADS):
        spot23 = jnp.where(at23 >= 8 * h, spot(at23 - 8 * h, h), spot23)
    put23 = jnp.where(iota((ROWS, 8 * HEADS), 0) == spot23, 1.0, 0.0).astype(BF)
    own1 = block_mask(64)
    own23 = block_mask(8)

    picks[0] = pick23
    barrier = pltpu.get_barrier_semaphore()
    peers = [(seq, other_head)]
    peers += [(sibling, head), (pair_peer[3], head), (cross_peer[3], head)]
    peers += [(chip_peer[d], head) for d in range(1, 8)]
    peers += [(z_peer[d], head) for d in range(1, 8)]
    for peer in peers:
        pl.semaphore_signal(barrier, inc=1, device_id=peer, device_id_type=MESH)
    pl.semaphore_wait(barrier, len(peers))

    picks_copy = push(picks.at[0], picks.at[1], head_s.at[4], head_r.at[4], seq, other_head)

    loads[0].wait()
    chosen_own = mm(pick23, tok[head]).astype(BF)
    picks_copy.wait_recv()
    rows_out[...] = mm(picks[1], tok[head]).astype(BF)
    rows_copy = push(rows_out, rows_in, head_s.at[5], head_r.at[5], seq, other_head)
    tok_copy = push(tok_hbm, tok.at[head], head_s.at[0], head_r.at[0], seq, other_head)

    def gout_push(n, rows):
        return push(
            gout_hbm.at[rows], gout.at[head, rows], head_s.at[n], head_r.at[n], seq, other_head
        )

    gout_copies = [gout_push(1, slice(0, 112))]
    loads[1].wait()

    def head_rows(which):
        return pl.ds(pl.multiple_of(which * HALF, HALF), HALF)

    small_own = [mm(chosen_own, wqkv[j, head_rows(head), :]) for j in (1, 2)]
    rows_copy.wait_recv()
    chosen_other = rows_in[...]
    for j in (1, 2):
        part = small_own[j - 1] + mm(chosen_other, wqkv[j, head_rows(other_head), :])
        part = by_head([part[8 * h : 8 * h + 8] for h in range(HEADS)])
        sv[j - 1] = part.astype(BF).astype(F32)
    sv_copy = push(sv.at[1 - core], sv_in, sib_s.at[0], sib_r.at[0], sibling)

    for j in range(3):
        cols = slice(WIDTH * j, WIDTH * (j + 1))
        acc[:, cols] = mm(tok[head], wqkv[j, pl.ds(pl.multiple_of(head * HALF, HALF), HALF), :])

    first = core == 0
    sv_copy.wait_recv()
    mine, theirs = sv[core], sv_in[...]
    kvz[0] = jnp.concatenate(
        [jnp.where(first, mine, theirs), jnp.where(first, theirs, mine)], 0
    ).astype(BF)
    kz_copies = [
        push(kvz.at[0], kvz.at[d], kz_s.at[d], kz_r.at[d], z_peer[d]) for d in FAR_FIRST
    ]
    loads[4].wait()
    for copy in kz_copies:
        copy.wait_recv()
    kvh[core, 0:80] = mm(comp[...], kvz[...].reshape(128, WIDTH)).astype(BF)
    kx_copies = []
    for d in (6, 5, 7, 4, 2, 1, 3):
        if d < 4:
            src, dst = kvh.at[core, 0:80], kvh.at[core, 80 * d : 80 * d + 80]
        else:
            src, dst = kvh.at[core, 64:80], kvh.at[core, 256 + 16 * d : 272 + 16 * d]
        kx_copies.append(push(src, dst, kx_s.at[d], kx_r.at[d], chip_peer[d]))
    gout_copies.append(gout_push(6, slice(112, ROWS)))

    tok_copy.wait_recv()
    for j in range(3):
        cols = slice(WIDTH * j, WIDTH * (j + 1))
        other_rows = pl.ds(pl.multiple_of(other_head * HALF, HALF), HALF)
        part = acc[:, cols] + mm(tok[other_head], wqkv[j, other_rows, :])
        if j == 0:
            part = part.astype(BF).astype(F32) * SCALE
        qkv[:, cols] = part.astype(BF)

    key_value = qkv[:, WIDTH:]
    picked1 = mm(pick1, key_value)
    kv1[0] = by_head([picked1[64 * h : 64 * h + 64] for h in range(HEADS)]).astype(BF)
    k1_copies = [
        push(kv1.at[0], kv1.at[d], k1_s.at[d], k1_r.at[d], pair_peer[d]) for d in range(1, 3)
    ]
    sib_tok_copy = push(tok.at[1 - core], sib_tok, sib_s.at[1], sib_r.at[1], sibling)

    q_block1 = jnp.where(own1, mm(pick1, qkv[:, :WIDTH]), 0.0).astype(BF)
    q_block23 = jnp.where(own23, mm(pick23, qkv[:, :WIDTH]), 0.0).astype(BF)

    low_lanes = iota((1, 128), 1) < 64
    side = [jnp.where(low_lanes, 1.0, 0.0).astype(BF), jnp.where(low_lanes, 0.0, 1.0).astype(BF)]

    def pair(start, p):
        return qkv[:, start + 128 * p : start + 128 * p + 128]

    def level0_forward(p):
        queries, keys, values = pair(0, p), pair(WIDTH, p), pair(2 * WIDTH, p)
        parts = []
        for e in range(2):
            weights = jnp.exp(mm(queries * side[e], keys, NT))
            w0[2 * p + e] = weights
            parts.append((mm(weights.astype(BF), values), jnp.sum(weights, axis=1, keepdims=True)))
        numer_ref[:, 128 * p : 128 * p + 128] = jnp.where(low_lanes, parts[0][0], parts[1][0])
        den_ref[:, 128 * p : 128 * p + 128] = jnp.where(low_lanes, parts[0][1], parts[1][1])

    level0_forward(0)

    level0_forward(1)
    for copy in kx_copies:
        copy.wait_recv()
    kvh_copy = push(kvh.at[core], kvh.at[core], sib_s.at[2], sib_r.at[2], sibling)
    level0_forward(2)

    k1_copies[1].wait_recv()
    k1_copies.append(push(kv1.at[2], kv1.at[3], k1_s.at[3], k1_r.at[3], sibling))
    k1_copies[0].wait_recv()
    k1_copies[2].wait_recv()
    keys1, values1 = kv1[:, :, :WIDTH].reshape(256, WIDTH), kv1[:, :, WIDTH:].reshape(256, WIDTH)
    weights, both = level_forward(q_block1, keys1, values1, own1, None)
    w1[...] = weights
    placed = place(put1, both)
    numer_ref[...] += placed[:, :WIDTH]
    den_ref[...] += placed[:, WIDTH:]

    loads[5].wait()
    sib_tok_copy.wait_recv()
    tok_t[:, :ROWS] = mm(perm[...], tok[core], NT).astype(BF)
    tok_t[:, ROWS:] = mm(perm[...], sib_tok[...], NT).astype(BF)

    loads[2].wait()
    loads[3].wait()
    for copy in gout_copies:
        copy.wait_recv()
    sib_gout_copy = push(gout.at[1 - core], sib_gout, sib_s.at[3], sib_r.at[3], sibling)
    grad_att = (mm(gout[0], wout[:, :HALF], NT) + mm(gout[1], wout[:, HALF:], NT)).astype(BF)
    gatt[...] = grad_att
    g_block1 = jnp.where(own1, mm(pick1, grad_att), 0.0).astype(BF)
    g_block23 = jnp.where(own23, mm(pick23, grad_att), 0.0).astype(BF)

    kvh_copy.wait_recv()
    keys23, values23 = kvh[0], kvh[1]
    small_row = lax.rem(iota((8 * HEADS, WIDTH), 0), 8)
    key_at = iota((8 * HEADS, WIDTH), 1)
    wide_key = (key_at >= 320) | (lax.rem(key_at, 80) >= 64)
    mask23 = jnp.where(wide_key, small_row, small_row + 8)
    mask23 = (mask23 == 4) | ((mask23 >= 8) & (mask23 < 12))
    weights, both = level_forward(q_block23, keys23, values23, own23, mask23)
    w23[...] = weights
    placed = place(put23, both)
    numer = numer_ref[...] + placed[:, :WIDTH]
    den = den_ref[...] + placed[:, WIDTH:]
    attended = (numer / den).astype(BF)
    att_buf[0] = attended
    att_copy = push(att_buf.at[0], att_buf.at[1], sib_s.at[4], sib_r.at[4], sibling)

    products = grad_att.astype(F32) * attended.astype(F32)
    stat_lane = iota((1, 128), 1)
    stats = jnp.zeros((ROWS, 128), F32)
    row_totals, deltas = [], []
    for h in range(HEADS):
        inv = den[:, 64 * h : 64 * h + 1]
        delta = jnp.sum(products[:, 64 * h : 64 * h + 64], axis=1, keepdims=True)
        row_totals.append(inv)
        deltas.append(delta)
        stats = jnp.where(stat_lane == h, inv, stats)
        stats = jnp.where(stat_lane == 8 + h, delta, stats)
    stats = jnp.concatenate(halves(stats), 1)

    def picked_stats(pick, rows_per_head):
        rows = HEADS * rows_per_head
        got = mm(pick, stats)
        got = got[:, :128] + got[:, 128:]
        at = iota((rows, 128), 0) // rows_per_head
        lanes = iota((rows, 128), 1)
        inv = jnp.sum(jnp.where(lanes == at, got, 0.0), axis=1, keepdims=True)
        delta = jnp.sum(jnp.where(lanes == at + 8, got, 0.0), axis=1, keepdims=True)
        return jnp.where(inv == 0.0, 1.0, inv), delta

    inv, delta = picked_stats(pick23, 8)
    grad_q23, grad_kv = level_backward(
        w23[...], q_block23, g_block23, keys23, values23, inv, delta, own23
    )
    grad_kv = grad_kv.astype(BF)
    gs[0] = grad_kv[:, :WIDTH]
    gs[1] = grad_kv[:, WIDTH:]
    gs_copy = push(gs.at[1 - core], gs_in, sib_s.at[5], sib_r.at[5], sibling)

    def out_cols(which):
        return pl.ds(pl.multiple_of(which * HALF, HALF), HALF)

    inv, delta = picked_stats(pick1, 64)
    grad_q1, grad_kv = level_backward(
        w1[...], q_block1, g_block1, keys1, values1, inv, delta, own1
    )
    gsend1[...] = grad_kv.astype(BF).reshape(4, 64, 2 * WIDTH)
    r1_copies = [
        push(gsend1.at[d], grecv1.at[d], r1_s.at[d], r1_r.at[d], sibling) for d in (1, 3)
    ]
    def level0_backward(p):
        queries, keys, values = pair(0, p), pair(WIDTH, p), pair(2 * WIDTH, p)
        grads = gatt[:, 128 * p : 128 * p + 128]
        parts = []
        for e in range(2):
            h = 2 * p + e
            probs = w0[h] / row_totals[h]
            grad_probs = mm(grads * side[e], values, NT)
            grad_scores = (probs * (grad_probs - deltas[h])).astype(BF)
            parts.append((
                mm(grad_scores, keys) * SCALE,
                mm(grad_scores, queries, TN),
                mm(probs.astype(BF), grads, TN),
            ))
        merged = [jnp.where(low_lanes, a, b) for a, b in zip(*parts)]
        cols = slice(128 * p, 128 * p + 128)
        gq_acc[:, cols] += merged[0]
        gkv_acc[:, cols] = merged[1]
        gkv_acc[:, WIDTH + 128 * p : WIDTH + 128 * p + 128] = merged[2]

    gq_acc[...] = place(put1, grad_q1) + place(put23, grad_q23)
    level0_backward(0)
    gs_copy.wait_recv()
    gx[...] = (gs[core].astype(F32) + gs_in[...].astype(F32)).astype(BF)

    def back_rows(d):
        return slice(80 * d, 80 * d + 80) if d < 4 else slice(256 + 16 * d, 272 + 16 * d)

    rx_copies = [
        push(gx.at[back_rows(d)], gx_in.at[back_rows(d)], rx_s.at[d], rx_r.at[d], chip_peer[d])
        for d in range(1, 8)
    ]
    def weight_term(left, own, other, arrived):
        term = mm(left[:, :ROWS], own)
        arrived.wait_recv()
        return term + mm(left[:, ROWS:], other[...])

    def y_block(d):
        return lax.rem(lax.div(chip_peer[d], 2), 4)

    def y_made(n, source, landing):
        return [
            made(source.at[y_block(d)], landing.at[d], y_s.at[n, d], y_r.at[n, d], chip_peer[d])
            for d in range(1, 4)
        ]

    def begin(copies):
        for copy in copies:
            copy.start()

    def y_send(n, source, landing):
        copies = y_made(n, source, landing)
        begin(copies)
        sent.extend(copies)
        return copies

    def y_total(own, landing):
        out = own.astype(F32)
        for d in range(1, 4):
            out = out + landing[d].astype(F32)
        return out

    def z_total(own, landing):
        out = own.astype(F32)
        for d in range(1, 8):
            out = out + landing[d].astype(F32)
        return out

    def arrive(copies):
        for copy in copies:
            copy.wait_recv()

    reducer = core == x_at
    x_copies = [
        made(ysend.at[n], xin.at[n], w_s.at[n], w_r.at[n], cross_peer[2]) for n in range(2)
    ]
    y_early = [y_made(n, ysend.at[n], yrecv.at[n]) for n in range(2)]

    def x_first(n, term):
        ysend[n] = term.astype(BF).reshape(4, 192, WIDTH)

        @pl.when(jnp.logical_not(reducer))
        def _():
            x_copies[n].start()

    def y_after_x(n):
        @pl.when(reducer)
        def _():
            x_copies[n].wait_recv()
            ysend[n] = (ysend[n].astype(F32) + xin[n].astype(F32)).astype(BF)
            begin(y_early[n])

    sib_gout_copy.wait_recv()
    gout_t[:, :ROWS] = mm(perm[...], gout[core], NT).astype(BF)
    gout_t[:, ROWS:] = mm(perm[...], sib_gout[...], NT).astype(BF)
    x_first(0, weight_term(gout_t, att_buf[0], att_buf.at[1], att_copy))

    level0_backward(1)
    level0_backward(2)
    part_a[...] = mm(attended, wout[:, out_cols(head)])
    grad_q = gq_acc[...].astype(BF)
    gbuf[0, 0] = grad_q
    gq_copy = push(gbuf.at[0, 0], gbuf.at[0, 1], sib_s.at[6], sib_r.at[6], sibling)

    for copy in rx_copies:
        copy.wait_recv()
    total = gx[0:80].astype(F32)
    for d in range(1, 4):
        total = total + gx_in[back_rows(d)].astype(F32)
    wide = total[64:80]
    for d in range(4, 8):
        wide = wide + gx_in[back_rows(d)].astype(F32)
    total = jnp.concatenate([total[:64], wide], 0).astype(BF)
    gz[...] = mm(comp[...], total, TN).astype(BF).reshape(8, 16, WIDTH)
    rz_copies = [
        push(gz.at[d], gz_in.at[d], rz_s.at[d], rz_r.at[d], z_peer[d]) for d in FAR_FIRST
    ]
    x_first(1, weight_term(tok_t, grad_q, gbuf.at[0, 1], gq_copy))
    mixed_out[...] = mm(attended, wout[:, out_cols(other_head)]).astype(BF)
    mixed_copy = push(mixed_out, mixed_in, head_s.at[3], head_r.at[3], seq, other_head)
    y_after_x(0)
    arrive(r1_copies)
    gsend1[2] = (gsend1[2].astype(F32) + grecv1[3].astype(F32)).astype(BF)
    r1_copies.append(push(gsend1.at[2], grecv1.at[2], r1_s.at[2], r1_r.at[2], pair_peer[2]))
    for copy in rz_copies:
        copy.wait_recv()
    total = gz[0].astype(F32)
    for d in range(1, 8):
        total = total + gz_in[d].astype(F32)
    gf[0] = total[:8]
    gf[1] = total[8:]
    gf_copy = push(gf.at[1 - core], gf_in, sib_s.at[7], sib_r.at[7], sibling)

    def tiled(x):
        return jnp.concatenate([x] * HEADS, 0)

    total = gsend1[0].astype(F32)
    r1_copies[2].wait_recv()
    for d in range(1, 3):
        total = total + grecv1[d].astype(F32)
    both1 = jnp.concatenate([own1, own1], 1)
    grad_kv = gkv_acc[...] + place(put1, jnp.where(both1, tiled(total), 0.0))
    gf_copy.wait_recv()
    mine, theirs = gf[core], gf_in[...]
    total = jnp.concatenate([jnp.where(first, mine, theirs), jnp.where(first, theirs, mine)], 1)
    both23 = jnp.concatenate([own23, own23], 1)
    grad_kv = grad_kv + place(put23, jnp.where(both23, tiled(total), 0.0))
    grad_kv = grad_kv.astype(BF)
    gbuf[1, 0] = grad_kv[:, :WIDTH]
    gbuf[2, 0] = grad_kv[:, WIDTH:]
    gk_copy = push(gbuf.at[1, 0], gbuf.at[1, 1], sib_s.at[8], sib_r.at[8], sibling)
    gv_copy = push(gbuf.at[2, 0], gbuf.at[2, 1], sib_s.at[9], sib_r.at[9], sibling)

    term_k = weight_term(tok_t, gbuf[1, 0], gbuf.at[1, 1], gk_copy)
    term_v = weight_term(tok_t, gbuf[2, 0], gbuf.at[2, 1], gv_copy)
    ysend_a[:, 0] = term_k[:, :256].astype(BF).reshape(4, 192, 256)
    ysend_a[:, 1] = term_v[:, :256].astype(BF).reshape(4, 192, 256)
    ya = y_send(2, ysend_a, yrecv_a)

    def z_made(n, source, landing):
        out = []
        for d in FAR_FIRST:
            block = lax.rem(lax.div(z_peer[d], 8), 8)
            out.append(made(source.at[block], landing.at[d], z_s.at[n, d], z_r.at[n, d], z_peer[d]))
        return out

    def z_send(n, source, landing):
        copies = z_made(n, source, landing)
        begin(copies)
        sent.extend(copies)
        return copies

    def z_blocks(pieces, m):
        return jnp.concatenate([piece[24 * m : 24 * m + 24] for piece in pieces], 0).astype(BF)

    quarters = [term[192 * n : 192 * n + 192, 256:] for term in (term_k, term_v) for n in range(4)]
    for m in range(8):
        zsend_b[m] = z_blocks(quarters, m)
    zb = z_send(2, zsend_b, zrecv_b)

    y_after_x(1)
    def token_part(which):
        out = mm(gbuf[0, 0], wqkv[0, head_rows(which), :], NT)
        out = out + mm(gbuf[1, 0], wqkv[1, head_rows(which), :], NT)
        return out + mm(gbuf[2, 0], wqkv[2, head_rows(which), :], NT)

    gtok_out[...] = token_part(other_head).astype(BF)
    gtok_copy = push(gtok_out, gtok_in, head_s.at[2], head_r.at[2], seq, other_head)

    own_tokens = token_part(head)
    arrive(ya)
    totals = y_total(ysend_a[y_at], yrecv_a)
    for m in range(8):
        zsend_a[m] = z_blocks([totals[0], totals[1]], m)
    za = z_send(1, zsend_a, zrecv_a)
    z_early = z_made(0, zsend, zrecv)
    f_copy = made(fbuf.at[0], fbuf.at[1], sib_s.at[10], sib_r.at[10], sibling)

    @pl.when(reducer)
    def _():
        arrive(y_early[0])
        arrive(y_early[1])
        totals = [y_total(ysend[p, y_at], yrecv.at[p]) for p in range(2)]
        for m in range(8):
            zsend[m] = z_blocks(totals, m)
        begin(z_early)

    arrive(zb)
    totals = z_total(zsend_b[z_at], zrecv_b)
    for n in range(4):
        ysend_b[n] = jnp.concatenate(
            [totals[24 * n : 24 * n + 24], totals[96 + 24 * n : 120 + 24 * n]], 0
        ).astype(BF)
    yb = y_send(3, ysend_b, yrecv_b)
    @pl.when(reducer)
    def _():
        arrive(z_early)
        fbuf[0] = z_total(zsend[z_at], zrecv)
        f_copy.start()

    gtok_copy.wait_recv()
    gtok_ref[...] = (own_tokens + gtok_in[...].astype(F32)).astype(BF)
    mixed_copy.wait_recv()
    mixed_ref[...] = (part_a[...] + mixed_in[...].astype(F32)).astype(BF)
    arrive(yb)
    xbuf[:, 256:] = y_total(ysend_b[y_at], yrecv_b)
    arrive(za)
    xbuf[:, :256] = z_total(zsend_a[z_at], zrecv_a)
    x1 = [
        push(xbuf, xrecv.at[d], x_s.at[d], x_r.at[d], cross_peer[d]) for d in range(1, 4)
    ]

    def finish(total):
        return [
            jnp.where(first, total[24 * n : 24 * n + 12], total[24 * n + 12 : 24 * n + 24])
            for n in range(2)
        ]

    @pl.when(jnp.logical_not(reducer))
    def _():
        f_copy.wait_recv()
        fbuf[0] = fbuf[1]

    one, two = finish(fbuf[0])
    gwout_ref[...] = one
    gqkv_ref[0] = two
    arrive(x1)
    straight = xbuf[...] + xrecv[2]
    crossed = xrecv[1] + xrecv[3]
    one, two = finish(jnp.where(reducer, straight, crossed))
    gqkv_ref[1] = one
    gqkv_ref[2] = two
    for copy in sent:
        copy.wait_send()

    @pl.when(reducer)
    def _():
        for copy in y_early[0] + y_early[1] + z_early + [f_copy]:
            copy.wait_send()

    @pl.when(jnp.logical_not(reducer))
    def _():
        for copy in x_copies:
            copy.wait_send()


def finish_kernel(mixed, gtok, gqkv, gwout, mixed_out, gtok_out, gqkv_out, gwout_out):
    mixed_out[...] = mixed[...]
    gtok_out[...] = gtok[...]
    gwout_out[...] = gwout[...]
    for j in range(3):
        gqkv_out[:, j, :] = gqkv[j]


def constants():
    at = np.arange(HALF)
    y, z, i = at // 192, at % 192 // 24, at % 24
    perm = np.zeros((HALF, HALF), np.float32)
    perm[at, z * 96 + y * 24 + i] = 1
    comp = np.zeros((80, 128), np.float32)
    for d in range(8):
        for e in range(2):
            for i in range(4):
                comp[8 * d + 4 * e + i, 16 * d + 8 * e + i] = 1
            comp[64 + 2 * d + e, 16 * d + 8 * e + 4] = 1
    return jnp.asarray(perm, BF), jnp.asarray(comp, BF)


def per_device(tokens, w_qkv, w_out, grad_out, offsets):
    perm, comp = constants()
    vm = pltpu.VMEM
    dma = pltpu.SemaphoreType.DMA
    scratch = [
        vm((2, ROWS, HALF), BF), vm((2, ROWS, HALF), BF), vm((3, 2 * HALF, WIDTH), BF),
        vm((WIDTH, 2 * HALF), BF), vm((HALF, HALF), BF), vm((80, 128), BF),
        vm((ROWS, HALF), BF), vm((ROWS, HALF), BF),
        vm((ROWS, 3 * WIDTH), F32), vm((ROWS, 3 * WIDTH), BF), vm((4, 64, 2 * WIDTH), BF),
        vm((2, 8, WIDTH), F32), vm((8, WIDTH), F32), vm((8, 16, WIDTH), BF),
        vm((2, WIDTH, WIDTH), BF),
        vm((HEADS, ROWS, ROWS), F32), vm((WIDTH, ROWS), F32), vm((8 * HEADS, WIDTH), F32),
        vm((ROWS, WIDTH), F32), vm((ROWS, WIDTH), F32), vm((ROWS, WIDTH), BF),
        vm((2, ROWS, WIDTH), BF), vm((ROWS, WIDTH), F32), vm((ROWS, 2 * WIDTH), F32),
        vm((HALF, 2 * ROWS), BF), vm((HALF, 2 * ROWS), BF), vm((3, 2, ROWS, WIDTH), BF),
        vm((4, 64, 2 * WIDTH), BF), vm((4, 64, 2 * WIDTH), BF),
        vm((2, WIDTH, WIDTH), BF), vm((WIDTH, WIDTH), BF),
        vm((WIDTH, WIDTH), BF), vm((WIDTH, WIDTH), BF),
        vm((8, 16, WIDTH), BF), vm((8, 16, WIDTH), BF),
        vm((2, 8, WIDTH), F32), vm((8, WIDTH), F32), vm((2, 48, ROWS), BF),
        vm((48, HALF), BF), vm((48, HALF), BF), vm((2, 4, 192, WIDTH), BF), vm((2, 48, WIDTH), F32),
        vm((ROWS, HALF), BF), vm((ROWS, HALF), BF), vm((ROWS, HALF), BF), vm((ROWS, HALF), BF),
        vm((ROWS, HALF), F32),
        vm((2, 4, 192, WIDTH), BF), vm((2, 4, 192, WIDTH), BF),
        vm((4, 2, 192, 256), BF), vm((4, 2, 192, 256), BF),
        vm((4, 48, 128), BF), vm((4, 48, 128), BF),
        vm((8, 48, WIDTH), BF), vm((8, 48, WIDTH), BF),
        vm((8, 48, 256), BF), vm((8, 48, 256), BF), vm((8, 192, 128), BF), vm((8, 192, 128), BF),
        vm((48, WIDTH), F32), vm((4, 48, WIDTH), F32),
        dma((6,)), dma((7,)), dma((7,)), dma((11,)), dma((11,)), dma((4,)), dma((4,)),
        dma((8,)), dma((8,)), dma((8,)), dma((8,)), dma((4,)), dma((4,)),
        dma((8,)), dma((8,)), dma((8,)), dma((8,)), dma((4, 4)), dma((4, 4)),
        dma((3, 8)), dma((3, 8)), dma((4,)), dma((4,)), dma((2,)), dma((2,)),
    ]
    anywhere = pl.BlockSpec(memory_space=pl.ANY)
    inside = pl.BlockSpec(memory_space=pltpu.VMEM)
    results = pl.pallas_call(
        kernel,
        out_shape=(
            jax.ShapeDtypeStruct((ROWS, HALF), BF),
            jax.ShapeDtypeStruct((ROWS, HALF), BF),
            jax.ShapeDtypeStruct((3, 12, WIDTH), F32),
            jax.ShapeDtypeStruct((12, WIDTH), F32),
        ),
        in_specs=[anywhere] * 6 + [pl.BlockSpec(memory_space=pltpu.SMEM)],
        out_specs=(inside,) * 4,
        scratch_shapes=scratch,
        compiler_params=pltpu.CompilerParams(
            collective_id=0, has_side_effects=True, vmem_limit_bytes=56 * 2**20
        ),
        cost_estimate=pl.CostEstimate(
            flops=8 * 10**9, bytes_accessed=12 * 2**20, transcendentals=600000
        ),
    )(tokens, grad_out, jnp.transpose(w_qkv, (1, 0, 2)), w_out, perm, comp, offsets)
    mixed, grad_tokens, grad_qkv, grad_w_out = pl.pallas_call(
        finish_kernel,
        out_shape=(
            jax.ShapeDtypeStruct((ROWS, HALF), BF),
            jax.ShapeDtypeStruct((ROWS, HALF), BF),
            jax.ShapeDtypeStruct((12, 3, WIDTH), F32),
            jax.ShapeDtypeStruct((12, WIDTH), F32),
        ),
        in_specs=[inside] * 4,
        out_specs=(inside,) * 4,
    )(*results)
    return mixed, grad_tokens, grad_qkv, jnp.transpose(grad_w_out)


def solution(mesh):
    placed = (
        P("seq", "head"),
        P(None, None, "head"),
        P("head", None),
        P("seq", "head"),
        P(None, "head"),
    )
    return jax.shard_map(
        per_device,
        mesh=mesh,
        in_specs=placed,
        out_specs=(P("seq", "head"), P("seq", "head"), P("seq", None, "head"), P("head", "seq")),
        check_vma=False,
    )
```
